256 devices in a mesh: dp: 64 (over x, z_lo, y, core), tensor: 4 (over z_hi).
Axes of the slice: x: 4, y: 4, z: 8 (z_hi: 4, z_lo: 2; z = z_hi * 2 + z_lo), core: 2. Of those that a mesh axis runs over, the one named last changes fastest.
Arguments:
- picture_embeds: bfloat16 [131072, 1152], P('dp', 'tensor'), may hold values from -6 to 6
- caption_embeds: bfloat16 [131072, 1152], P(('dp', 'tensor')), may hold values from -6 to 6
- starting_caption_slab: int32 [], replicated, may hold values from 0 to 63
- score_multiplier: float32 [], replicated, may hold values from 5 to 20
- score_offset: float32 [], replicated, may hold values from -4 to -2
Outputs:
- image_grad: bfloat16 [131072, 1152], P('dp', 'tensor')
- text_grad: float32 [2, 4, 512, 1152], P(None, 'tensor', 'dp')
The draws below stay inside these ranges and needn't reach their ends.
All inputs are finite; a program needn't handle non-finite values.
Results may differ from the reference program's by a relative error of at most 0.0058.
Values may be sent and summed in bfloat16 or wider, within the bound.
No kernel may reach another device: no remote copies, remote signals or barrier semaphores. Data moves between devices by JAX's collectives and lax.ppermute only.
A program may use at most 64 MiB of HBM per device.

```python
import math
import jax
import jax.numpy as jnp
from jax import lax

D = 1152
ROWS = 512
STEPS = 2
GROUP = 4
BLOCKS = 64
BATCH = 131072


def shard_levels(stream_key, shape, shards, least, top_value):
    gain, own = 1.0, jax.random.fold_in(stream_key, 6)
    for position, blocks in shards:
        heights = jnp.exp(jax.random.uniform(jax.random.fold_in(own, position), (blocks,), jnp.float32, least / len(shards), top_value / len(shards)))
        gain = gain * jnp.repeat(heights, shape[position] // blocks).reshape([-1 if axis == position else 1 for axis in range(len(shape))])
    return gain


def bell_draw(own_key, shape, spread, limit, pieces=(), kind=jnp.bfloat16):
    entries = jax.random.normal(own_key, shape, jnp.float32) * spread
    if len(pieces) > 0:
        entries = shard_levels(own_key, shape, pieces, -0.22, 0.18) * entries
    return jnp.clip(entries, min=-limit, max=limit).astype(kind)


def setup_inputs(seed: int = 0) -> dict:
    key_of = jax.random.split(jax.random.key(seed), 6)
    return {
        "picture_embeds": bell_draw(key_of[0], (BATCH, D), 1.0, 6.0, ((0, 64), (1, 4))),
        "caption_embeds": bell_draw(key_of[1], (BATCH, D), 1.0, 6.0, ((0, 256),)),
        "starting_caption_slab": jax.random.randint(key_of[2], (), 0, BLOCKS).astype(jnp.int32),
        "score_multiplier": jnp.clip(jnp.exp(jax.random.uniform(key_of[3], (), jnp.float32, math.log(5.0), math.log(20.0))), 5.0, 20.0),
        "score_offset": jnp.clip(jax.random.uniform(key_of[4], (), jnp.float32, -4.0, -2.0), -4.0, -2.0),
    }


epsilon = 1e-06

def unit_rows(values):
    widened = values.astype(jnp.float32)
    return widened * lax.rsqrt(lax.optimization_barrier(jnp.sum(widened * widened, axis=-1, keepdims=True)) + epsilon)

def reference(picture_embeds, caption_embeds, starting_caption_slab, score_multiplier, score_offset):
    images = unit_rows(picture_embeds).astype(jnp.bfloat16).reshape(BLOCKS, GROUP, ROWS, D)
    captions = unit_rows(caption_embeds).astype(jnp.bfloat16).reshape(BLOCKS, GROUP, ROWS, D)
    identity = jnp.eye(ROWS, dtype=jnp.float32)
    image_sum = jnp.zeros((BLOCKS, GROUP, ROWS, D), jnp.float32)
    text_steps = []
    for step_index in range(STEPS):
        holder_index = ((starting_caption_slab + step_index) % BLOCKS).astype(jnp.int32)
        present_caption_slab = lax.dynamic_index_in_dim(captions, holder_index, 0, keepdims=False).astype(jnp.float32)

        def per_group(operands):
            group_images, group_index = operands
            replicated_picture_embeds = group_images.astype(jnp.float32)
            similarity_scores = score_multiplier * jnp.einsum('nud,nrd->nur', replicated_picture_embeds, present_caption_slab) + score_offset
            matching_labels = jnp.where(group_index == holder_index, 1.0, 0.0).astype(jnp.float32) * identity
            parameters_halfwidth = ((jax.nn.sigmoid(similarity_scores) - matching_labels) * score_multiplier).astype(jnp.bfloat16).astype(jnp.float32)
            image_term = jnp.einsum('kij,kjd->kid', parameters_halfwidth, present_caption_slab)
            text_term = jnp.einsum('kij,kid->kjd', parameters_halfwidth, replicated_picture_embeds)
            return (image_term, text_term)
        image_term, text_term = lax.map(per_group, (images, jnp.arange(BLOCKS, dtype=jnp.int32)))
        image_sum = image_sum + image_term
        text_steps.append(lax.optimization_barrier(jnp.sum(text_term, axis=0)))
    image_grad = image_sum.astype(jnp.bfloat16).reshape(BLOCKS * GROUP * ROWS, D)
    return (image_grad, jnp.stack(text_steps))
```

```python
import jax
import jax.numpy as jnp
from jax import lax
from jax.sharding import Mesh
from jax.sharding import PartitionSpec as P

EPSILON = 1e-06
SIZES = (("x", 4), ("zl", 2), ("y", 4), ("c", 2), ("t", 4))
DP = ("x", "zl", "y", "c")


def shift(value, axis, by, size):
    return lax.ppermute(value, axis, [(i, (i + by) % size) for i in range(size)])


def unit(values, axis):
    widened = values.astype(jnp.float32)
    total = jnp.sum(widened * widened, axis=axis, keepdims=True)
    return (widened * lax.rsqrt(total + EPSILON)).astype(jnp.bfloat16)


def pick(parts, index):
    return lax.dynamic_index_in_dim(parts, index, 0, keepdims=False)


def exchange_width(parts):
    mine = lax.axis_index("t")
    got = [pick(parts, mine)]
    for by in (3, 2, 1):
        got.append(shift(pick(parts, (mine + by) % 4), "t", by, 4))
    ring = jnp.concatenate(got + got)
    start = (4 - mine) % 4
    size = parts.shape[1]
    return lax.dynamic_slice_in_dim(ring, start * size, 4 * size, 0)


def across(parts):
    return lax.all_to_all(parts, ("x", "y"), split_axis=0, concat_axis=0, tiled=True)


def per_device(pictures, captions, start, multiplier, offset):
    f32, bf16 = jnp.float32, jnp.bfloat16
    width = captions.shape[1]
    core, z_lo = lax.axis_index("c"), lax.axis_index("zl")
    place = lax.axis_index(DP)

    step_of = (start ^ core) & 1
    holders = [(start + step_of) % 64, (start + (1 - step_of)) % 64]
    chip = holders[0] >> 1
    root_y, root_z, root_x = chip & 3, (chip >> 2) & 1, chip >> 3

    text = captions.reshape(4, 2, 4, 16, width).transpose(0, 2, 1, 3, 4).reshape(16, 32, width)
    wide = pictures.reshape(4, 512, 288).transpose(0, 2, 1)
    images = unit(exchange_width(wide), 0)

    piece = pick(across(text), root_x * 4 + root_y)
    other = shift(piece, "zl", 1, 2)
    piece = unit(jnp.where(z_lo == root_z, piece, other), 1)
    own = across(jnp.broadcast_to(piece[None], (16, 32, width))).reshape(512, width)
    slabs = [own, shift(own, "c", 1, 2)]

    place_of = jnp.arange(512, dtype=jnp.int32)
    row = ((((place_of >> 7) * 2 + ((place_of >> 4) & 1)) * 4 + ((place_of >> 5) & 3)) << 4) + (place_of & 15)
    same = row[:, None] == jnp.arange(512, dtype=jnp.int32)[None, :]

    grad, terms = 0.0, []
    for slab, holder in zip(slabs, holders):
        logits = multiplier * jnp.dot(slab, images, preferred_element_type=f32) + offset
        positive = (same & (place == holder)).astype(f32)
        weights = ((jax.nn.sigmoid(logits) - positive) * multiplier).astype(bf16)
        grad = grad + lax.dot_general(slab, weights, (((0,), (0,)), ((), ())), preferred_element_type=f32)
        terms.append(lax.dot_general(weights, images, (((1,), (1,)), ((), ())), preferred_element_type=f32))

    back = exchange_width(grad.astype(bf16).reshape(4, 288, 512)).reshape(4, 288, 512)
    image_grad = back.transpose(0, 2, 1).reshape(2048, 288)

    total = terms[0] + shift(terms[1].astype(bf16), "c", 1, 2).astype(f32)
    total = jnp.sum(across(total.astype(bf16).reshape(16, 32, width)).astype(f32), axis=0)
    total = total.reshape(2, 16, width)
    total = pick(total, z_lo) + shift(pick(total, 1 - z_lo), "zl", 1, 2)
    total = total.reshape(2, 8, width)
    mine, theirs = pick(total, core), shift(pick(total, 1 - core), "c", 1, 2)
    first = step_of == 0
    text_grad = jnp.stack([jnp.where(first, mine, theirs), jnp.where(first, theirs, mine)])
    return image_grad, text_grad[:, None]


def solution(mesh):
    names, sizes = zip(*SIZES)
    grid = Mesh(mesh.devices.reshape(sizes), names)
    return jax.shard_map(
        per_device,
        mesh=grid,
        in_specs=(P(DP, "t"), P(names, None), P(), P(), P()),
        out_specs=(P(DP, "t"), P(None, "t", DP, None)),
        check_vma=False,
    )
```

```python
import jax
import jax.numpy as jnp
from jax import lax
from jax.experimental import pallas as pl
from jax.experimental.pallas import tpu as pltpu
from jax.sharding import Mesh
from jax.sharding import PartitionSpec as P

EPSILON = 1e-06
SIZES = (("x", 4), ("zl", 2), ("y", 4), ("c", 2), ("t", 4))
DP = ("x", "zl", "y", "c")
D, ROWS, PART, PEERS = 1152, 512, 288, 4
F32, BF16 = jnp.float32, jnp.bfloat16
VMEM, SMEM = pl.BlockSpec(memory_space=pltpu.VMEM), pl.BlockSpec(memory_space=pltpu.SMEM)
PARAMS = pltpu.CompilerParams(vmem_limit_bytes=24 << 20)


def like(*shape, dtype=BF16):
    return jax.ShapeDtypeStruct(shape, dtype)


def shift(value, axis, by, size):
    return lax.ppermute(value, axis, [(i, (i + by) % size) for i in range(size)])


def pick(parts, index):
    return lax.dynamic_index_in_dim(parts, index, 0, keepdims=False)


def across(parts):
    return lax.all_to_all(parts, ("x", "y"), split_axis=0, concat_axis=0, tiled=True)


def exchange_width(pieces):
    return [pieces[0]] + [shift(pieces[d], "t", d, PEERS) for d in (1, 2, 3)]


def cut_kernel(pictures, *pieces):
    mine = lax.axis_index("t")
    for d, piece in enumerate(pieces):
        block = lax.rem(mine + d, PEERS)
        rows = pl.ds(pl.multiple_of(block * ROWS, ROWS), ROWS)
        piece[...] = pictures[rows, :].T


def cut(pictures):
    return pl.pallas_call(
        cut_kernel,
        out_shape=[like(PART, ROWS)] * PEERS,
        in_specs=[VMEM],
        out_specs=[VMEM] * PEERS,
        compiler_params=PARAMS,
        cost_estimate=pl.CostEstimate(flops=0, bytes_accessed=3 << 20, transcendentals=0),
    )(pictures)


def unit_kernel(*refs):
    pieces, out = refs[:PEERS], refs[PEERS]
    mine = lax.axis_index("t")
    total = jnp.zeros((1, ROWS), F32)
    for piece in pieces:
        wide = piece[...].astype(F32)
        total = total + jnp.sum(wide * wide, axis=0, keepdims=True)
    scale = lax.rsqrt(total + EPSILON)
    for d, piece in enumerate(pieces):
        source = lax.rem(mine + (PEERS - d), PEERS)
        rows = pl.ds(pl.multiple_of(source * PART, PART), PART)
        out[rows, :] = (piece[...].astype(F32) * scale).astype(BF16)


def unit_columns(pieces):
    return pl.pallas_call(
        unit_kernel,
        out_shape=like(D, ROWS),
        in_specs=[VMEM] * PEERS,
        out_specs=VMEM,
        compiler_params=PARAMS,
        cost_estimate=pl.CostEstimate(flops=3 << 20, bytes_accessed=3 << 20, transcendentals=0),
    )(*pieces)


def unit_rows(values):
    wide = values.astype(F32)
    total = jnp.sum(wide * wide, axis=1, keepdims=True)
    return (wide * lax.rsqrt(total + EPSILON)).astype(BF16)


def place():
    axis = lax.axis_index
    return ((axis("x") * 2 + axis("zl")) * 4 + axis("y")) * 2 + axis("c")


def slab_weights(other, start, multiplier, offset, text, images, weights):
    core = lax.axis_index("c")
    step = (start[0] + core + other) & 1
    holder = lax.rem(start[0] + step, 64)
    held = place() == holder
    times, plus = multiplier[0], offset[0]
    tile = 128
    for at in range(0, ROWS, tile):
        logits = times * jnp.dot(text[at : at + tile, :], images[...], preferred_element_type=F32) + plus
        spot = lax.broadcasted_iota(jnp.int32, (tile, ROWS), 0) + at
        row = ((((spot >> 7) * 2 + ((spot >> 4) & 1)) * 4 + ((spot >> 5) & 3)) << 4) + (spot & 15)
        same = row == lax.broadcasted_iota(jnp.int32, (tile, ROWS), 1)
        positive = jnp.where(same & held, 1.0, 0.0)
        weights[at : at + tile, :] = ((jax.nn.sigmoid(logits) - positive) * times).astype(BF16)


def own_kernel(start, multiplier, offset, text, images, grad, terms, weights):
    slab_weights(0, start, multiplier, offset, text, images, weights)
    terms[...] = lax.dot_general(weights[...], images[...], (((1,), (1,)), ((), ())), preferred_element_type=F32)
    grad[...] = lax.dot_general(text[...], weights[...], (((0,), (0,)), ((), ())), preferred_element_type=F32)


def other_kernel(start, multiplier, offset, text, images, before, terms, *refs):
    pieces, (weights, grad) = refs[:PEERS], refs[PEERS:]
    mine = lax.axis_index("t")
    slab_weights(1, start, multiplier, offset, text, images, weights)
    terms[...] = lax.dot_general(
        weights[...], images[...], (((1,), (1,)), ((), ())), preferred_element_type=F32
    ).astype(BF16)
    grad[...] = before[...] + lax.dot_general(
        text[...], weights[...], (((0,), (0,)), ((), ())), preferred_element_type=F32
    )
    for d, piece in enumerate(pieces):
        target = lax.rem(mine + d, PEERS)
        piece[...] = grad[pl.ds(pl.multiple_of(target * PART, PART), PART), :].astype(BF16)


COST = pl.CostEstimate(flops=6 * D * ROWS * ROWS, bytes_accessed=8 << 20, transcendentals=ROWS * ROWS)


def own_slab(scalars, text, images):
    return pl.pallas_call(
        own_kernel,
        out_shape=[like(D, ROWS, dtype=F32), like(ROWS, D, dtype=F32)],
        in_specs=[SMEM] * 3 + [VMEM] * 2,
        out_specs=[VMEM] * 2,
        scratch_shapes=[pltpu.VMEM((ROWS, ROWS), BF16)],
        compiler_params=PARAMS,
        cost_estimate=COST,
    )(*scalars, text, images)


def other_slab(scalars, text, images, before):
    return pl.pallas_call(
        other_kernel,
        out_shape=[like(ROWS, D)] + [like(PART, ROWS)] * PEERS,
        in_specs=[SMEM] * 3 + [VMEM] * 3,
        out_specs=[VMEM] * (1 + PEERS),
        scratch_shapes=[pltpu.VMEM((ROWS, ROWS), BF16), pltpu.VMEM((D, ROWS), F32)],
        compiler_params=PARAMS,
        cost_estimate=COST,
    )(*scalars, text, images, before)


def lay_kernel(*refs):
    pieces, out = refs[:PEERS], refs[PEERS]
    mine = lax.axis_index("t")
    for d, piece in enumerate(pieces):
        block = lax.rem(mine + (PEERS - d), PEERS)
        out[pl.ds(pl.multiple_of(block * ROWS, ROWS), ROWS), :] = piece[...].T


def lay(pieces):
    return pl.pallas_call(
        lay_kernel,
        out_shape=like(PEERS * ROWS, PART),
        in_specs=[VMEM] * PEERS,
        out_specs=VMEM,
        compiler_params=PARAMS,
        cost_estimate=pl.CostEstimate(flops=0, bytes_accessed=3 << 20, transcendentals=0),
    )(*pieces)


def per_device(pictures, captions, start, multiplier, offset):
    core, z_lo = lax.axis_index("c"), lax.axis_index("zl")

    step_of = (start ^ core) & 1
    chip = ((start + step_of) % 64) >> 1
    root_y, root_z, root_x = chip & 3, (chip >> 2) & 1, chip >> 3

    pieces = cut(pictures)
    captions, pieces = lax.optimization_barrier((captions, pieces))
    text = captions.reshape(4, 2, 4, 16, D).transpose(0, 2, 1, 3, 4).reshape(16, 32, D)
    arrived = exchange_width(pieces)

    piece = pick(across(text), root_x * 4 + root_y)
    other = shift(piece, "zl", 1, 2)
    piece = unit_rows(jnp.where(z_lo == root_z, piece, other))
    piece, arrived = lax.optimization_barrier((piece, arrived))
    own = across(jnp.broadcast_to(piece[None], (16, 32, D))).reshape(ROWS, D)
    images = unit_columns(arrived)

    scalars = [value.reshape(1) for value in (start, multiplier, offset)]
    grad, own_terms = own_slab(scalars, own, images)
    other_terms, *pieces = other_slab(scalars, shift(own, "c", 1, 2), images, grad)

    image_grad = lay(exchange_width(pieces))

    total = own_terms + shift(other_terms, "c", 1, 2).astype(F32)
    total = jnp.sum(across(total.astype(BF16).reshape(16, 32, D)).astype(F32), axis=0)
    total = total.reshape(2, 2, 8, D)
    near, far = pick(total, z_lo), pick(total, 1 - z_lo)

    def flip(value, z, c):
        pairs = [(i, i ^ (8 * z + c)) for i in range(16)]
        return lax.ppermute(value, ("zl", "y", "c"), pairs)

    mine = pick(near, core) + flip(pick(far, core), 1, 0)
    theirs = flip(pick(near, 1 - core), 0, 1) + flip(pick(far, 1 - core), 1, 1)
    first = step_of == 0
    text_grad = jnp.stack([jnp.where(first, mine, theirs), jnp.where(first, theirs, mine)])
    return image_grad, text_grad[:, None]


def solution(mesh):
    names, sizes = zip(*SIZES)
    grid = Mesh(mesh.devices.reshape(sizes), names)
    return jax.shard_map(
        per_device,
        mesh=grid,
        in_specs=(P(DP, "t"), P(names, None), P(), P(), P()),
        out_specs=(P(DP, "t"), P(None, "t", DP, None)),
        check_vma=False,
    )
```

```python
import jax
import jax.numpy as jnp
from jax import lax
from jax.experimental import pallas as pl
from jax.experimental.pallas import tpu as pltpu
from jax.sharding import Mesh
from jax.sharding import PartitionSpec as P

EPSILON = 1e-06
SIZES = (("x", 4), ("zl", 2), ("y", 4), ("c", 2), ("t", 4))
DP = ("x", "zl", "y", "c")
D, ROWS, PART, PEERS = 1152, 512, 288, 4
F32, BF16 = jnp.float32, jnp.bfloat16
VMEM, SMEM, HBM = (pl.BlockSpec(memory_space=space) for space in (pltpu.VMEM, pltpu.SMEM, pltpu.HBM))
PARAMS = pltpu.CompilerParams(vmem_limit_bytes=24 << 20)


def like(*shape, dtype=BF16):
    return jax.ShapeDtypeStruct(shape, dtype)


def shift(value, axis, by, size):
    return lax.ppermute(value, axis, [(i, (i + by) % size) for i in range(size)])


def pick(parts, index):
    return lax.dynamic_index_in_dim(parts, index, 0, keepdims=False)


def across(parts):
    return lax.all_to_all(parts, ("x", "y"), split_axis=0, concat_axis=0, tiled=True)


def exchange_width(pieces):
    return [pieces[0]] + [shift(pieces[d], "t", d, PEERS) for d in (1, 2, 3)]


def cut_kernel(pictures, *refs):
    pieces, done = refs[:PEERS], refs[PEERS]
    mine = lax.axis_index("t")
    copies = []
    for d, piece in enumerate(pieces):
        block = lax.rem(mine + d, PEERS)
        rows = pl.ds(pl.multiple_of(block * ROWS, ROWS), ROWS)
        copies.append(pltpu.make_async_copy(pictures.at[:, rows], piece, done.at[d]))
        copies[-1].start()
    for copy in copies:
        copy.wait()


def cut(pictures):
    return pl.pallas_call(
        cut_kernel,
        out_shape=[like(PART, ROWS)] * PEERS,
        in_specs=[HBM],
        out_specs=[VMEM] * PEERS,
        scratch_shapes=[pltpu.SemaphoreType.DMA((PEERS,))],
        compiler_params=PARAMS,
        cost_estimate=pl.CostEstimate(flops=0, bytes_accessed=3 << 20, transcendentals=0),
    )(pictures)


def unit_kernel(*refs):
    pieces, out = refs[:PEERS], refs[PEERS]
    mine = lax.axis_index("t")
    total = jnp.zeros((1, ROWS), F32)
    for piece in pieces:
        wide = piece[...].astype(F32)
        total = total + jnp.sum(wide * wide, axis=0, keepdims=True)
    scale = lax.rsqrt(total + EPSILON)
    for d, piece in enumerate(pieces):
        source = lax.rem(mine + (PEERS - d), PEERS)
        rows = pl.ds(pl.multiple_of(source * PART, PART), PART)
        out[rows, :] = (piece[...].astype(F32) * scale).astype(BF16)


def unit_columns(pieces):
    return pl.pallas_call(
        unit_kernel,
        out_shape=like(D, ROWS),
        in_specs=[VMEM] * PEERS,
        out_specs=VMEM,
        compiler_params=PARAMS,
        cost_estimate=pl.CostEstimate(flops=3 << 20, bytes_accessed=3 << 20, transcendentals=0),
    )(*pieces)


def unit_rows(values):
    wide = values.astype(F32)
    total = jnp.sum(wide * wide, axis=1, keepdims=True)
    return (wide * lax.rsqrt(total + EPSILON)).astype(BF16)


def place():
    axis = lax.axis_index
    return ((axis("x") * 2 + axis("zl")) * 4 + axis("y")) * 2 + axis("c")


def slab_weights(other, start, multiplier, offset, text, images, weights):
    core = lax.axis_index("c")
    step = (start[0] + core + other) & 1
    holder = lax.rem(start[0] + step, 64)
    held = place() == holder
    times, plus = multiplier[0], offset[0]
    tile = 128
    for at in range(0, ROWS, tile):
        logits = times * jnp.dot(text[at : at + tile, :], images[...], preferred_element_type=F32) + plus
        row = lax.broadcasted_iota(jnp.int32, (tile, ROWS), 0) + at
        same = row == lax.broadcasted_iota(jnp.int32, (tile, ROWS), 1)
        positive = jnp.where(same & held, 1.0, 0.0)
        weights[at : at + tile, :] = ((jax.nn.sigmoid(logits) - positive) * times).astype(BF16)


def slab_terms(images, weights, by_owner, keep, send):
    core = lax.axis_index("c")
    tile = 128
    for at in range(0, ROWS, tile):
        terms = lax.dot_general(
            weights[at : at + tile, :], images[...], (((1,), (1,)), ((), ())), preferred_element_type=F32
        )
        for inner in range(tile // 8):
            group = at // 8 + inner
            x, z, y, c = group >> 4, (group >> 3) & 1, (group >> 1) & 3, group & 1
            by_owner[c, x * 4 + y, 8 * z : 8 * z + 8, :] = terms[8 * inner : 8 * inner + 8, :]
    keep[...] = by_owner[core]
    send[...] = by_owner[1 - core].astype(BF16)


def own_kernel(start, multiplier, offset, text, images, keep, send, grad, weights, by_owner):
    slab_weights(0, start, multiplier, offset, text, images, weights)
    slab_terms(images, weights, by_owner, keep, send)
    grad[...] = lax.dot_general(text[...], weights[...], (((0,), (0,)), ((), ())), preferred_element_type=F32)


def other_kernel(start, multiplier, offset, text, images, keep, send, weights, by_owner):
    slab_weights(1, start, multiplier, offset, text, images, weights)
    slab_terms(images, weights, by_owner, keep, send)


def pieces_kernel(text, weights, before, *refs):
    pieces, grad = refs[:PEERS], refs[PEERS]
    mine = lax.axis_index("t")
    grad[...] = before[...] + lax.dot_general(
        text[...], weights[...], (((0,), (0,)), ((), ())), preferred_element_type=F32
    )
    for d, piece in enumerate(pieces):
        target = lax.rem(mine + d, PEERS)
        piece[...] = grad[pl.ds(pl.multiple_of(target * PART, PART), PART), :].astype(BF16)


def cost(products, moved):
    return pl.CostEstimate(flops=2 * products * D * ROWS * ROWS, bytes_accessed=moved << 20, transcendentals=0)


OWNED = (16, 16, D)


def own_slab(scalars, text, images):
    return pl.pallas_call(
        own_kernel,
        out_shape=[like(*OWNED, dtype=F32), like(*OWNED), like(D, ROWS, dtype=F32)],
        in_specs=[SMEM] * 3 + [VMEM] * 2,
        out_specs=[VMEM] * 3,
        scratch_shapes=[pltpu.VMEM((ROWS, ROWS), BF16), pltpu.VMEM((2,) + OWNED, F32)],
        compiler_params=PARAMS,
        cost_estimate=cost(3, 8),
    )(*scalars, text, images)


def other_slab(scalars, text, images):
    return pl.pallas_call(
        other_kernel,
        out_shape=[like(*OWNED, dtype=F32), like(*OWNED), like(ROWS, ROWS)],
        in_specs=[SMEM] * 3 + [VMEM] * 2,
        out_specs=[VMEM] * 3,
        scratch_shapes=[pltpu.VMEM((2,) + OWNED, F32)],
        compiler_params=PARAMS,
        cost_estimate=cost(2, 5),
    )(*scalars, text, images)


def image_pieces(text, weights, before):
    return pl.pallas_call(
        pieces_kernel,
        out_shape=[like(PART, ROWS)] * PEERS,
        in_specs=[VMEM] * 3,
        out_specs=[VMEM] * PEERS,
        scratch_shapes=[pltpu.VMEM((D, ROWS), F32)],
        compiler_params=PARAMS,
        cost_estimate=cost(1, 5),
    )(text, weights, before)


def join_kernel(own, from_other, other, from_own, out):
    out[:, :16, :] = (own[...] + from_other[...].astype(F32)).astype(BF16)
    out[:, 16:, :] = (other[...] + from_own[...].astype(F32)).astype(BF16)


def join(own, from_other, other, from_own):
    return pl.pallas_call(
        join_kernel,
        out_shape=like(16, 32, D),
        in_specs=[VMEM] * 4,
        out_specs=VMEM,
        compiler_params=PARAMS,
        cost_estimate=cost(0, 4),
    )(own, from_other, other, from_own)


def sum_kernel(start, parts, keep, send, total):
    z_lo = lax.axis_index("zl")
    first = (start[0] + lax.axis_index("c")) & 1
    total[...] = jnp.sum(parts[...].astype(F32), axis=0)
    for slab, step in ((0, first), (1, 1 - first)):
        keep[step] = total[pl.ds(pl.multiple_of(16 * slab + 8 * z_lo, 8), 8), :]
        send[step] = total[pl.ds(pl.multiple_of(16 * slab + 8 * (1 - z_lo), 8), 8), :]


def sum_chips(start, parts):
    return pl.pallas_call(
        sum_kernel,
        out_shape=[like(2, 8, D, dtype=F32)] * 2,
        in_specs=[SMEM, VMEM],
        out_specs=[VMEM] * 2,
        scratch_shapes=[pltpu.VMEM((32, D), F32)],
        compiler_params=PARAMS,
        cost_estimate=cost(0, 1),
    )(start, parts)


def lay_kernel(*refs):
    pieces, out, done = refs[:PEERS], refs[PEERS], refs[PEERS + 1]
    mine = lax.axis_index("t")
    copies = []
    for d, piece in enumerate(pieces):
        block = lax.rem(mine + (PEERS - d), PEERS)
        rows = pl.ds(pl.multiple_of(block * ROWS, ROWS), ROWS)
        copies.append(pltpu.make_async_copy(piece, out.at[:, rows], done.at[d]))
        copies[-1].start()
    for copy in copies:
        copy.wait()


def lay(pieces):
    return pl.pallas_call(
        lay_kernel,
        out_shape=like(PART, PEERS * ROWS),
        in_specs=[VMEM] * PEERS,
        out_specs=HBM,
        scratch_shapes=[pltpu.SemaphoreType.DMA((PEERS,))],
        compiler_params=PARAMS,
        cost_estimate=cost(0, 3),
    )(*pieces)


def per_device(pictures, captions, start, multiplier, offset):
    core, z_lo = lax.axis_index("c"), lax.axis_index("zl")

    step_of = (start ^ core) & 1
    chip = ((start + step_of) % 64) >> 1
    root_y, root_z, root_x = chip & 3, (chip >> 2) & 1, chip >> 3

    arrived = exchange_width(cut(pictures.T))
    text = across(captions.reshape(16, 32, D))
    text, arrived[1], arrived[3] = lax.optimization_barrier((text, arrived[1], arrived[3]))

    piece = pick(text, root_x * 4 + root_y)
    other = shift(piece, "zl", 1, 2)
    piece = unit_rows(jnp.where(z_lo == root_z, piece, other))
    own = across(jnp.broadcast_to(piece[None], (16, 32, D))).reshape(ROWS, D)
    own, arrived[2] = lax.optimization_barrier((own, arrived[2]))
    images = unit_columns(arrived)

    scalars = [value.reshape(1) for value in (start, multiplier, offset)]
    keep_own, send_own, grad = own_slab(scalars, own, images)
    theirs = shift(own, "c", 1, 2)
    keep_other, send_other, weights = other_slab(scalars, theirs, images)
    image_grad = lay(exchange_width(image_pieces(theirs, weights, grad))).T

    parts = join(keep_own, shift(send_other, "c", 1, 2), keep_other, shift(send_own, "c", 1, 2))
    keep, send = sum_chips(scalars[0], across(parts))
    text_grad = keep + shift(send, "zl", 1, 2)
    return image_grad, text_grad[:, None]


def solution(mesh):
    names, sizes = zip(*SIZES)
    grid = Mesh(mesh.devices.reshape(sizes), names)
    return jax.shard_map(
        per_device,
        mesh=grid,
        in_specs=(P(DP, "t"), P(names, None), P(), P(), P()),
        out_specs=(P(DP, "t"), P(None, "t", DP, None)),
        check_vma=False,
    )
```

```python
import jax
import jax.numpy as jnp
from jax import lax
from jax.experimental import pallas as pl
from jax.experimental.pallas import tpu as pltpu
from jax.sharding import Mesh
from jax.sharding import PartitionSpec as P

EPSILON = 1e-06
SIZES = (("x", 4), ("zl", 2), ("y", 4), ("c", 2), ("t", 4))
DP = ("x", "zl", "y", "c")
D, ROWS, PART, PEERS = 1152, 512, 288, 4
CHUNK, PIECE, HALF = 128, 32, 256
OWNED = (16, 16, D)
F32, BF16 = jnp.float32, jnp.bfloat16
VMEM, SMEM, HBM = (pl.BlockSpec(memory_space=space) for space in (pltpu.VMEM, pltpu.SMEM, pltpu.HBM))
DMA = pltpu.SemaphoreType.DMA


def like(*shape, dtype=BF16):
    return jax.ShapeDtypeStruct(shape, dtype)


def call(kernel, outs, ins, scratch=(), products=0, moved=1):
    single = not isinstance(outs, list)
    return pl.pallas_call(
        kernel,
        out_shape=outs,
        in_specs=ins,
        out_specs=VMEM if single else [VMEM] * len(outs),
        scratch_shapes=list(scratch),
        compiler_params=pltpu.CompilerParams(vmem_limit_bytes=16 << 20),
        cost_estimate=pl.CostEstimate(
            flops=2 * products * D * ROWS * ROWS, bytes_accessed=moved << 20, transcendentals=0
        ),
    )


def shift(value, axis, by, size):
    return lax.ppermute(value, axis, [(i, (i + by) % size) for i in range(size)])


def along(value, first, by):
    pairs = []
    for i in range(64):
        x, z, y, c = i >> 4, (i >> 3) & 1, (i >> 1) & 3, i & 1
        if (c == 0) == first:
            x = (x + by) % 4
        else:
            y = (y + by) % 4
        pairs.append((i, ((x * 2 + z) * 4 + y) * 2 + c))
    return lax.ppermute(value, DP, pairs)


def spot():
    x, y, c = lax.axis_index("x"), lax.axis_index("y"), lax.axis_index("c")
    return c, jnp.where(c == 0, x, y), jnp.where(c == 0, y, x)


def holder_of(start, other):
    step = (start[0] + lax.axis_index("c") + other) & 1
    return step, lax.rem(start[0] + step, 64)


def back(place, d):
    return lax.rem(place + (4 - d), 4)


def ahead(place, d):
    return lax.rem(place + d, 4)


def window(index, size):
    return pl.ds(pl.multiple_of(index * size, size), size)


def run(copies):
    for copy in copies:
        copy.start()
    for copy in copies:
        copy.wait()


def cut_kernel(pictures, own, one, three, two_low, two_high, done):
    mine = lax.axis_index("t")
    places = [(own, 0, 0), (one, 1, 0), (three, 3, 0), (two_low, 2, 0), (two_high, 2, HALF)]
    copies = []
    for i, (piece, d, at) in enumerate(places):
        size = piece.shape[1]
        rows = pl.ds(pl.multiple_of(ahead(mine, d) * ROWS + at, HALF), size)
        copies.append(pltpu.make_async_copy(pictures.at[:, rows], piece, done.at[i]))
    run(copies)


def arrange_kernel(captions, text, done):
    run(
        [
            pltpu.make_async_copy(captions.at[x, z], text.at[x, :, z], done.at[2 * x + z])
            for x in range(4)
            for z in range(2)
        ]
    )


def pick_kernel(start, parts, piece):
    chip = holder_of(start, 0)[1] >> 1
    piece[...] = parts[(chip >> 3) * 4 + (chip & 3)]


def unit_rows_kernel(start, here, there, piece):
    chip = holder_of(start, 0)[1] >> 1
    is_here = ((chip >> 2) & 1) == lax.axis_index("zl")
    wide = jnp.where(is_here, here[...].astype(F32), there[...].astype(F32))
    total = jnp.sum(wide * wide, axis=1, keepdims=True)
    piece[...] = (wide * lax.rsqrt(total + EPSILON)).astype(BF16)


def gather_kernel(*refs):
    chunk = refs[4]
    place = spot()[2]
    for d in range(4):
        chunk[window(back(place, d), PIECE), :] = refs[d][...]


def unit_columns_kernel(own, one, three, two_low, two_high, out):
    mine = lax.axis_index("t")
    total = [jnp.zeros((1, HALF), F32)] * 2
    parts = []
    for d, low, high in ((0, own, own), (1, one, one), (3, three, three), (2, two_low, two_high)):
        for side, piece in enumerate((low, high)):
            at = side * HALF if piece.shape[1] == ROWS else 0
            parts.append((d, side, piece, at))
            wide = piece[:, at : at + HALF].astype(F32)
            total[side] = total[side] + jnp.sum(wide * wide, axis=0, keepdims=True)
    scale = [lax.rsqrt(value + EPSILON) for value in total]
    for d, side, piece, at in parts:
        wide = piece[:, at : at + HALF].astype(F32)
        out[window(back(mine, d), PART), side * HALF : side * HALF + HALF] = (wide * scale[side]).astype(BF16)


def slab_weights(other, start, multiplier, offset, chunks, images, text, weights):
    core, first, second = spot()
    held = lax.axis_index(DP) == holder_of(start, other)[1]
    kind, place = (core, first) if other == 0 else (1 - core, second)
    times, plus = multiplier[0], offset[0]
    for d in range(4):
        rows = slice(CHUNK * d, CHUNK * d + CHUNK)
        text[rows, :] = chunks[d][...]
        logits = times * jnp.dot(chunks[d][...], images[...], preferred_element_type=F32) + plus
        at = lax.broadcasted_iota(jnp.int32, (CHUNK, 1), 0)
        inner, along_first = at >> 5, back(place, d)
        x = jnp.where(kind == 0, along_first, inner)
        y = jnp.where(kind == 0, inner, along_first)
        row = x * 128 + ((at >> 4) & 1) * 64 + y * 16 + (at & 15)
        same = row == lax.broadcasted_iota(jnp.int32, (CHUNK, ROWS), 1)
        positive = jnp.where(same & held, 1.0, 0.0)
        weights[rows, :] = ((jax.nn.sigmoid(logits) - positive) * times).astype(BF16)


def slab_terms(other, images, weights, by_owner, keep, send):
    core, first, second = spot()
    kind, place = (core, first) if other == 0 else (1 - core, second)
    for d in range(4):
        terms = lax.dot_general(
            weights[CHUNK * d : CHUNK * d + CHUNK, :],
            images[...],
            (((1,), (1,)), ((), ())),
            preferred_element_type=F32,
        )
        for inner in range(4):
            straight, turned = back(place, d) * 4 + inner, inner * 4 + back(place, d)
            spots = (jnp.where(kind == 0, straight, turned), jnp.where(kind == 0, turned, straight))
            for z in range(2):
                for c in range(2):
                    at = PIECE * inner + 16 * z + 8 * c
                    by_owner[c, spots[c], 8 * z : 8 * z + 8, :] = terms[at : at + 8, :]
    keep[...] = by_owner[core]
    send[...] = by_owner[1 - core].astype(BF16)


def turned_product(text, weights):
    return lax.dot_general(text[...], weights[...], (((0,), (0,)), ((), ())), preferred_element_type=F32)


def own_kernel(start, multiplier, offset, *refs):
    chunks, (images, keep, send, grad, text, weights, by_owner) = refs[:4], refs[4:]
    slab_weights(0, start, multiplier, offset, chunks, images, text, weights)
    slab_terms(0, images, weights, by_owner, keep, send)
    grad[...] = turned_product(text, weights)


def other_kernel(start, multiplier, offset, *refs):
    chunks, (images, keep, send, weights, text, by_owner) = refs[:4], refs[4:]
    slab_weights(1, start, multiplier, offset, chunks, images, text, weights)
    slab_terms(1, images, weights, by_owner, keep, send)


def pieces_kernel(*refs):
    chunks, (weights, before), pieces, (text, grad) = refs[:4], refs[4:6], refs[6:10], refs[10:]
    for d in range(4):
        text[CHUNK * d : CHUNK * d + CHUNK, :] = chunks[d][...]
    mine = lax.axis_index("t")
    grad[...] = before[...] + turned_product(text, weights)
    for d, piece in enumerate(pieces):
        piece[...] = grad[window(ahead(mine, d), PART), :].astype(BF16)


def join_kernel(own, from_other, other, from_own, *outs):
    place = spot()[1]
    for d, out in enumerate(outs):
        rows = window(ahead(place, d), 4)
        out[:, :16, :] = (own[rows] + from_other[rows].astype(F32)).astype(out.dtype)
        out[:, 16:, :] = (other[rows] + from_own[rows].astype(F32)).astype(out.dtype)


def first_sum_kernel(own, one, two, three, *refs):
    outs, total = refs[:4], refs[4]
    place = spot()[2]
    total[...] = (own[...] + one[...].astype(F32)) + (two[...].astype(F32) + three[...].astype(F32))
    for d, out in enumerate(outs):
        out[...] = total[ahead(place, d)].astype(out.dtype)


def second_sum_kernel(start, own, one, two, three, keep, send, total):
    z_lo = lax.axis_index("zl")
    step = holder_of(start, 0)[0]
    total[...] = (own[...] + one[...].astype(F32)) + (two[...].astype(F32) + three[...].astype(F32))
    for slab, at in ((0, step), (1, 1 - step)):
        keep[at] = total[window(2 * slab + z_lo, 8), :]
        send[at] = total[window(2 * slab + 1 - z_lo, 8), :]


def lay_kernel(*refs):
    pieces, out, done = refs[:4], refs[4], refs[5]
    mine = lax.axis_index("t")
    run(
        [
            pltpu.make_async_copy(piece, out.at[:, window(back(mine, d), ROWS)], done.at[d])
            for d, piece in enumerate(pieces)
        ]
    )


def lay(pieces):
    return pl.pallas_call(
        lay_kernel,
        out_shape=like(PART, PEERS * ROWS),
        in_specs=[VMEM] * PEERS,
        out_specs=HBM,
        scratch_shapes=[DMA((PEERS,))],
    )(*pieces)


def per_device(pictures, captions, start, multiplier, offset):
    start, multiplier, offset = (value.reshape(1) for value in (start, multiplier, offset))
    scalars, scalar_specs = (start, multiplier, offset), [SMEM] * 3

    shapes = [like(PART, ROWS)] * 3 + [like(PART, HALF)] * 2
    near, one, three, low, high = call(cut_kernel, shapes, [HBM], [DMA((5,))], moved=2)(pictures.T)
    one, three, low, high = (shift(v, "t", d, PEERS) for v, d in ((one, 1), (three, 3), (low, 2), (high, 2)))

    text = call(arrange_kernel, like(4, 4, 2, 16, D), [HBM], [DMA((8,))], moved=2)(captions.reshape(4, 2, 4, 16, D))
    text = lax.all_to_all(text.reshape(16, PIECE, D), ("x", "y"), split_axis=0, concat_axis=0, tiled=True)
    text, one, three, low = lax.optimization_barrier((text, one, three, low))
    piece = call(pick_kernel, like(PIECE, D), [SMEM, VMEM])(start, text)
    piece = call(unit_rows_kernel, like(PIECE, D), [SMEM] + [VMEM] * 2)(start, piece, shift(piece, "zl", 1, 2))

    pieces = [piece] + [along(piece, False, d) for d in (1, 2, 3)]
    chunk = call(gather_kernel, like(CHUNK, D), [VMEM] * 4)(*pieces)
    own = [chunk] + [along(chunk, True, d) for d in (1, 2, 3)]
    *own, high = lax.optimization_barrier((*own, high))
    theirs = [shift(chunk, "c", 1, 2) for chunk in own]
    images = call(unit_columns_kernel, like(D, ROWS), [VMEM] * 5, moved=3)(near, one, three, low, high)

    text_scratch, owner_scratch = pltpu.VMEM((ROWS, D), BF16), pltpu.VMEM((2,) + OWNED, F32)
    kept, sent, square = like(*OWNED, dtype=F32), like(*OWNED), like(ROWS, ROWS)
    keep_own, send_own, grad = call(
        own_kernel,
        [kept, sent, like(D, ROWS, dtype=F32)],
        scalar_specs + [VMEM] * 5,
        [text_scratch, pltpu.VMEM((ROWS, ROWS), BF16), owner_scratch],
        products=3,
        moved=8,
    )(*scalars, *own, images)
    keep_other, send_other, weights = call(
        other_kernel,
        [kept, sent, square],
        scalar_specs + [VMEM] * 5,
        [text_scratch, owner_scratch],
        products=2,
        moved=5,
    )(*scalars, *theirs, images)
    pieces = call(
        pieces_kernel,
        [like(PART, ROWS)] * PEERS,
        [VMEM] * 6,
        [text_scratch, pltpu.VMEM((D, ROWS), F32)],
        products=1,
        moved=5,
    )(*theirs, weights, grad)
    *pieces, keep_own = lax.optimization_barrier((*pieces, keep_own))
    returned = [pieces[0]] + [shift(pieces[d], "t", d, PEERS) for d in (1, 2, 3)]

    parts = call(
        join_kernel, [like(4, PIECE, D, dtype=F32)] + [like(4, PIECE, D)] * 3, [VMEM] * 4, moved=4
    )(keep_own, shift(send_other, "c", 1, 2), keep_other, shift(send_own, "c", 1, 2))
    parts = [parts[0]] + [along(parts[d], True, d) for d in (1, 2, 3)]
    *parts, returned[1], returned[3] = lax.optimization_barrier((*parts, returned[1], returned[3]))
    parts = call(
        first_sum_kernel,
        [like(PIECE, D, dtype=F32)] + [like(PIECE, D)] * 3,
        [VMEM] * 4,
        [pltpu.VMEM((4, PIECE, D), F32)],
    )(*parts)
    parts = [parts[0]] + [along(parts[d], False, d) for d in (1, 2, 3)]
    keep, send = call(
        second_sum_kernel, [like(2, 8, D, dtype=F32)] * 2, [SMEM] + [VMEM] * 4, [pltpu.VMEM((PIECE, D), F32)]
    )(start, *parts)
    text_grad = keep + shift(send, "zl", 1, 2)
    return lay(returned).T, text_grad[:, None]


def solution(mesh):
    names, sizes = zip(*SIZES)
    grid = Mesh(mesh.devices.reshape(sizes), names)
    return jax.shard_map(
        per_device,
        mesh=grid,
        in_specs=(P(DP, "t"), P(names, None), P(), P(), P()),
        out_specs=(P(DP, "t"), P(None, "t", DP, None)),
        check_vma=False,
    )
```

```python
import jax
import jax.numpy as jnp
from jax import lax
from jax.experimental import pallas as pl
from jax.experimental.pallas import tpu as pltpu
from jax.sharding import Mesh
from jax.sharding import PartitionSpec as P

EPSILON = 1e-06
SIZES = (("x", 4), ("zl", 2), ("y", 4), ("c", 2), ("t", 4))
DP = ("x", "zl", "y", "c")
D, ROWS, PART, PEERS = 1152, 512, 288, 4
CHUNK, PIECE, HALF = 128, 32, 256
OWNED = (16, 16, D)
F32, BF16 = jnp.float32, jnp.bfloat16
VMEM, SMEM, HBM = (pl.BlockSpec(memory_space=space) for space in (pltpu.VMEM, pltpu.SMEM, pltpu.HBM))
DMA = pltpu.SemaphoreType.DMA


def like(*shape, dtype=BF16):
    return jax.ShapeDtypeStruct(shape, dtype)


def call(kernel, outs, ins, scratch=(), products=0, moved=1):
    single = not isinstance(outs, list)
    return pl.pallas_call(
        kernel,
        out_shape=outs,
        in_specs=ins,
        out_specs=VMEM if single else [VMEM] * len(outs),
        scratch_shapes=list(scratch),
        compiler_params=pltpu.CompilerParams(vmem_limit_bytes=16 << 20),
        cost_estimate=pl.CostEstimate(
            flops=2 * products * D * ROWS * ROWS, bytes_accessed=moved << 20, transcendentals=0
        ),
    )


def shift(value, axis, by, size):
    return lax.ppermute(value, axis, [(i, (i + by) % size) for i in range(size)])


def along(value, first, by):
    pairs = []
    for i in range(64):
        x, z, y, c = i >> 4, (i >> 3) & 1, (i >> 1) & 3, i & 1
        if (c == 0) == first:
            x = (x + by) % 4
        else:
            y = (y + by) % 4
        pairs.append((i, ((x * 2 + z) * 4 + y) * 2 + c))
    return lax.ppermute(value, DP, pairs)


def spot():
    x, y, c = lax.axis_index("x"), lax.axis_index("y"), lax.axis_index("c")
    return c, jnp.where(c == 0, x, y), jnp.where(c == 0, y, x)


def holder_of(start, other):
    step = (start[0] + lax.axis_index("c") + other) & 1
    return step, lax.rem(start[0] + step, 64)


def back(place, d):
    return lax.rem(place + (4 - d), 4)


def ahead(place, d):
    return lax.rem(place + d, 4)


def window(index, size):
    return pl.ds(pl.multiple_of(index * size, size), size)


def run(copies):
    for copy in copies:
        copy.start()
    for copy in copies:
        copy.wait()


def cut_kernel(pictures, own, one, three, two_low, two_high, done):
    mine = lax.axis_index("t")
    places = [(own, 0, 0), (one, 1, 0), (three, 3, 0), (two_low, 2, 0), (two_high, 2, HALF)]
    copies = []
    for i, (piece, d, at) in enumerate(places):
        size = piece.shape[1]
        rows = pl.ds(pl.multiple_of(ahead(mine, d) * ROWS + at, HALF), size)
        copies.append(pltpu.make_async_copy(pictures.at[:, rows], piece, done.at[i]))
    run(copies)


def pick_kernel(start, parts, piece):
    chip = holder_of(start, 0)[1] >> 1
    piece[...] = parts[(chip >> 3) * 4 + (chip & 3)]


def unit_rows_kernel(start, here, there, piece):
    chip = holder_of(start, 0)[1] >> 1
    is_here = ((chip >> 2) & 1) == lax.axis_index("zl")
    wide = jnp.where(is_here, here[...].astype(F32), there[...].astype(F32))
    total = jnp.sum(wide * wide, axis=1, keepdims=True)
    piece[...] = (wide * lax.rsqrt(total + EPSILON)).astype(BF16)


def gather_kernel(*refs):
    chunk = refs[4]
    place = spot()[2]
    for d in range(4):
        chunk[window(back(place, d), PIECE), :] = refs[d][...]


def unit_columns_kernel(own, one, three, two_low, two_high, out):
    mine = lax.axis_index("t")
    total = [jnp.zeros((1, HALF), F32)] * 2
    parts = []
    for d, low, high in ((0, own, own), (1, one, one), (3, three, three), (2, two_low, two_high)):
        for side, piece in enumerate((low, high)):
            at = side * HALF if piece.shape[1] == ROWS else 0
            parts.append((d, side, piece, at))
            wide = piece[:, at : at + HALF].astype(F32)
            total[side] = total[side] + jnp.sum(wide * wide, axis=0, keepdims=True)
    scale = [lax.rsqrt(value + EPSILON) for value in total]
    for d, side, piece, at in parts:
        wide = piece[:, at : at + HALF].astype(F32)
        out[window(back(mine, d), PART), side * HALF : side * HALF + HALF] = (wide * scale[side]).astype(BF16)


def slab_weights(other, start, multiplier, offset, chunks, images, text, weights):
    core, first, second = spot()
    held = lax.axis_index(DP) == holder_of(start, other)[1]
    kind, place = (core, first) if other == 0 else (1 - core, second)
    times, plus = multiplier[0], offset[0]
    for d in range(4):
        rows = slice(CHUNK * d, CHUNK * d + CHUNK)
        text[rows, :] = chunks[d][...]
        logits = times * jnp.dot(chunks[d][...], images[...], preferred_element_type=F32) + plus
        at = lax.broadcasted_iota(jnp.int32, (CHUNK, 1), 0)
        inner, along_first = at >> 5, back(place, d)
        x = jnp.where(kind == 0, along_first, inner)
        y = jnp.where(kind == 0, inner, along_first)
        row = x * 128 + y * PIECE + (at & (PIECE - 1))
        same = row == lax.broadcasted_iota(jnp.int32, (CHUNK, ROWS), 1)
        positive = jnp.where(same & held, 1.0, 0.0)
        weights[rows, :] = ((jax.nn.sigmoid(logits) - positive) * times).astype(BF16)


def slab_terms(other, images, weights, by_owner, keep, send):
    core, first, second = spot()
    kind, place = (core, first) if other == 0 else (1 - core, second)
    for d in range(4):
        terms = lax.dot_general(
            weights[CHUNK * d : CHUNK * d + CHUNK, :],
            images[...],
            (((1,), (1,)), ((), ())),
            preferred_element_type=F32,
        )
        for inner in range(4):
            outer = back(place, d)
            x = jnp.where(kind == 0, outer, inner)
            part = jnp.where(kind == 0, inner, outer)
            rows = pl.ds(pl.multiple_of((part >> 1) * 8, 8), 8)
            for low in range(2):
                y = (part & 1) * 2 + low
                spots = (x * 4 + y, y * 4 + x)
                for c in range(2):
                    at = PIECE * inner + 16 * low + 8 * c
                    by_owner[c, spots[c], rows, :] = terms[at : at + 8, :]
    keep[...] = by_owner[core]
    send[...] = by_owner[1 - core].astype(BF16)


def turned_product(text, weights):
    return lax.dot_general(text[...], weights[...], (((0,), (0,)), ((), ())), preferred_element_type=F32)


def own_kernel(start, multiplier, offset, *refs):
    chunks, (images, keep, send, grad, text, weights, by_owner) = refs[:4], refs[4:]
    slab_weights(0, start, multiplier, offset, chunks, images, text, weights)
    slab_terms(0, images, weights, by_owner, keep, send)
    grad[...] = turned_product(text, weights)


def other_kernel(start, multiplier, offset, *refs):
    chunks, (images, keep, send, weights, text, by_owner) = refs[:4], refs[4:]
    slab_weights(1, start, multiplier, offset, chunks, images, text, weights)
    slab_terms(1, images, weights, by_owner, keep, send)


def pieces_kernel(*refs):
    chunks, (weights, before), pieces, (text, grad) = refs[:4], refs[4:6], refs[6:10], refs[10:]
    for d in range(4):
        text[CHUNK * d : CHUNK * d + CHUNK, :] = chunks[d][...]
    mine = lax.axis_index("t")
    grad[...] = before[...] + turned_product(text, weights)
    for d, piece in enumerate(pieces):
        piece[...] = grad[window(ahead(mine, d), PART), :].astype(BF16)


def join_kernel(own, from_other, other, from_own, *outs):
    place = spot()[1]
    for d, out in enumerate(outs):
        rows = window(ahead(place, d), 4)
        out[:, :16, :] = (own[rows] + from_other[rows].astype(F32)).astype(out.dtype)
        out[:, 16:, :] = (other[rows] + from_own[rows].astype(F32)).astype(out.dtype)


def first_sum_kernel(own, one, two, three, *refs):
    outs, total = refs[:4], refs[4]
    place = spot()[2]
    total[...] = (own[...] + one[...].astype(F32)) + (two[...].astype(F32) + three[...].astype(F32))
    for d, out in enumerate(outs):
        out[...] = total[ahead(place, d)].astype(out.dtype)


def second_sum_kernel(start, own, one, two, three, keep, send, total):
    z_lo = lax.axis_index("zl")
    step = holder_of(start, 0)[0]
    total[...] = (own[...] + one[...].astype(F32)) + (two[...].astype(F32) + three[...].astype(F32))
    for slab, at in ((0, step), (1, 1 - step)):
        keep[at] = total[window(2 * slab + z_lo, 8), :]
        send[at] = total[window(2 * slab + 1 - z_lo, 8), :]


def lay_copies(places, out, done):
    mine = lax.axis_index("t")
    run(
        [
            pltpu.make_async_copy(piece, out.at[:, window(back(mine, d), ROWS)], done.at[i])
            for i, (d, piece) in enumerate(places)
        ]
    )


def lay_near_kernel(own, one, three, out, done):
    lay_copies([(0, own), (1, one), (3, three)], out, done)


def lay_far_kernel(two, before, out, done):
    lay_copies([(2, two)], out, done)


def lay_near(own, one, three):
    return pl.pallas_call(
        lay_near_kernel,
        out_shape=like(PART, PEERS * ROWS),
        in_specs=[VMEM] * 3,
        out_specs=HBM,
        scratch_shapes=[DMA((3,))],
    )(own, one, three)


def lay_far(two, before):
    return pl.pallas_call(
        lay_far_kernel,
        out_shape=like(PART, PEERS * ROWS),
        in_specs=[VMEM, HBM],
        out_specs=HBM,
        scratch_shapes=[DMA((1,))],
        input_output_aliases={1: 0},
    )(two, before)


def per_device(pictures, captions, start, multiplier, offset):
    start, multiplier, offset = (value.reshape(1) for value in (start, multiplier, offset))
    scalars, scalar_specs = (start, multiplier, offset), [SMEM] * 3

    shapes = [like(PART, ROWS)] * 3 + [like(PART, HALF)] * 2
    near, one, three, low, high = call(cut_kernel, shapes, [HBM], [DMA((5,))], moved=2)(pictures.T)
    one, three, low, high = (shift(v, "t", d, PEERS) for v, d in ((one, 1), (three, 3), (low, 2), (high, 2)))

    text = lax.all_to_all(captions.reshape(16, PIECE, D), ("x", "y"), split_axis=0, concat_axis=0, tiled=True)
    text, one, three = lax.optimization_barrier((text, one, three))
    piece = call(pick_kernel, like(PIECE, D), [SMEM, VMEM])(start, text)
    piece = call(unit_rows_kernel, like(PIECE, D), [SMEM] + [VMEM] * 2)(start, piece, shift(piece, "zl", 1, 2))

    pieces = [piece] + [along(piece, False, d) for d in (1, 2, 3)]
    *pieces, low = lax.optimization_barrier((*pieces, low))
    chunk = call(gather_kernel, like(CHUNK, D), [VMEM] * 4)(*pieces)
    own = [chunk] + [along(chunk, True, d) for d in (1, 2, 3)]
    *own, high = lax.optimization_barrier((*own, high))
    theirs = [shift(chunk, "c", 1, 2) for chunk in own]
    images = call(unit_columns_kernel, like(D, ROWS), [VMEM] * 5, moved=3)(near, one, three, low, high)

    text_scratch, owner_scratch = pltpu.VMEM((ROWS, D), BF16), pltpu.VMEM((2,) + OWNED, F32)
    kept, sent, square = like(*OWNED, dtype=F32), like(*OWNED), like(ROWS, ROWS)
    keep_own, send_own, grad = call(
        own_kernel,
        [kept, sent, like(D, ROWS, dtype=F32)],
        scalar_specs + [VMEM] * 5,
        [text_scratch, pltpu.VMEM((ROWS, ROWS), BF16), owner_scratch],
        products=3,
        moved=8,
    )(*scalars, *own, images)
    keep_other, send_other, weights = call(
        other_kernel,
        [kept, sent, square],
        scalar_specs + [VMEM] * 5,
        [text_scratch, owner_scratch],
        products=2,
        moved=5,
    )(*scalars, *theirs, images)
    pieces = call(
        pieces_kernel,
        [like(PART, ROWS)] * PEERS,
        [VMEM] * 6,
        [text_scratch, pltpu.VMEM((D, ROWS), F32)],
        products=1,
        moved=5,
    )(*theirs, weights, grad)
    *pieces, keep_own = lax.optimization_barrier((*pieces, keep_own))
    returned = [pieces[0]] + [shift(pieces[d], "t", d, PEERS) for d in (1, 2, 3)]

    parts = call(
        join_kernel, [like(4, PIECE, D, dtype=F32)] + [like(4, PIECE, D)] * 3, [VMEM] * 4, moved=4
    )(keep_own, shift(send_other, "c", 1, 2), keep_other, shift(send_own, "c", 1, 2))
    parts = [parts[0]] + [along(parts[d], True, d) for d in (1, 2, 3)]
    *parts, returned[1], returned[3] = lax.optimization_barrier((*parts, returned[1], returned[3]))
    parts = call(
        first_sum_kernel,
        [like(PIECE, D, dtype=F32)] + [like(PIECE, D)] * 3,
        [VMEM] * 4,
        [pltpu.VMEM((4, PIECE, D), F32)],
    )(*parts)
    parts = [parts[0]] + [along(parts[d], False, d) for d in (1, 2, 3)]
    keep, send = call(
        second_sum_kernel, [like(2, 8, D, dtype=F32)] * 2, [SMEM] + [VMEM] * 4, [pltpu.VMEM((PIECE, D), F32)]
    )(start, *parts)
    text_grad = keep + shift(send, "zl", 1, 2)
    image_grad = lay_far(returned[2], lay_near(returned[0], returned[1], returned[3]))
    return image_grad.T, text_grad[:, None]


def solution(mesh):
    names, sizes = zip(*SIZES)
    grid = Mesh(mesh.devices.reshape(sizes), names)
    return jax.shard_map(
        per_device,
        mesh=grid,
        in_specs=(P(DP, "t"), P(names, None), P(), P(), P()),
        out_specs=(P(DP, "t"), P(None, "t", DP, None)),
        check_vma=False,
    )
```

```python
import jax
import jax.numpy as jnp
from jax import lax
from jax.experimental import pallas as pl
from jax.experimental.pallas import tpu as pltpu
from jax.sharding import Mesh
from jax.sharding import PartitionSpec as P

EPSILON = 1e-06
SIZES = (("x", 4), ("zl", 2), ("y", 4), ("c", 2), ("t", 4))
DP = ("x", "zl", "y", "c")
D, ROWS, PART, PEERS = 1152, 512, 288, 4
CHUNK, PIECE, HALF = 128, 32, 256
OWNED = (16, 16, D)
F32, BF16 = jnp.float32, jnp.bfloat16
VMEM, SMEM, HBM = (pl.BlockSpec(memory_space=space) for space in (pltpu.VMEM, pltpu.SMEM, pltpu.HBM))
DMA = pltpu.SemaphoreType.DMA


def like(*shape, dtype=BF16):
    return jax.ShapeDtypeStruct(shape, dtype)


def call(kernel, outs, ins, scratch=(), products=0, moved=1, vmem=16 << 20):
    single = not isinstance(outs, list)
    return pl.pallas_call(
        kernel,
        out_shape=outs,
        in_specs=ins,
        out_specs=VMEM if single else [VMEM] * len(outs),
        scratch_shapes=list(scratch),
        compiler_params=pltpu.CompilerParams(vmem_limit_bytes=vmem),
        cost_estimate=pl.CostEstimate(
            flops=2 * products * D * ROWS * ROWS, bytes_accessed=moved << 20, transcendentals=0
        ),
    )


def shift(value, axis, by, size):
    return lax.ppermute(value, axis, [(i, (i + by) % size) for i in range(size)])


def along(value, first, by):
    pairs = []
    for i in range(64):
        x, z, y, c = i >> 4, (i >> 3) & 1, (i >> 1) & 3, i & 1
        if (c == 0) == first:
            x = (x + by) % 4
        else:
            y = (y + by) % 4
        pairs.append((i, ((x * 2 + z) * 4 + y) * 2 + c))
    return lax.ppermute(value, DP, pairs)


def spot():
    x, y, c = lax.axis_index("x"), lax.axis_index("y"), lax.axis_index("c")
    return c, jnp.where(c == 0, x, y), jnp.where(c == 0, y, x)


def holder_of(start, other):
    step = (start[0] + lax.axis_index("c") + other) & 1
    return step, lax.rem(start[0] + step, 64)


def back(place, d):
    return lax.rem(place + (4 - d), 4)


def ahead(place, d):
    return lax.rem(place + d, 4)


def window(index, size):
    return pl.ds(pl.multiple_of(index * size, size), size)


def run(copies):
    for copy in copies:
        copy.start()
    for copy in copies:
        copy.wait()


def cut_pieces(places, pictures, done):
    mine = lax.axis_index("t")
    copies = []
    for i, (piece, d, at) in enumerate(places):
        size = piece.shape[1]
        rows = pl.ds(pl.multiple_of(ahead(mine, d) * ROWS + at, HALF), size)
        copies.append(pltpu.make_async_copy(pictures.at[:, rows], piece, done.at[i]))
    run(copies)


def cut_kernel(captions, pictures, *refs):
    chunks, (own, one, three, text_done, done) = refs[:4], refs[4:]
    place = spot()[1]
    copies = [
        pltpu.make_async_copy(captions.at[ahead(place, d)], chunk, text_done.at[d]) for d, chunk in enumerate(chunks)
    ]
    for copy in copies:
        copy.start()
    cut_pieces([(own, 0, 0), (one, 1, 0), (three, 3, 0)], pictures, done)
    for copy in copies:
        copy.wait()


def cut_far_kernel(pictures, low, high, done):
    cut_pieces([(low, 2, 0), (high, 2, HALF)], pictures, done)


def root_of(start):
    chip = holder_of(start, 0)[1] >> 1
    x, y, core = chip >> 3, chip & 3, lax.axis_index("c")
    return jnp.where(core == 0, x, y), jnp.where(core == 0, y, x), (chip >> 2) & 1


def first_pick_kernel(start, *refs):
    chunks, outs = refs[:4], refs[4:]
    _, first, second = spot()
    came = lax.rem(first + 4 - root_of(start)[0], 4)
    for d, chunk in enumerate(chunks):

        @pl.when(came == d)
        def _():
            for by, out in enumerate(outs):
                out[...] = chunk[ahead(second, by)]


def second_pick_kernel(start, *refs):
    pieces, out = refs[:4], refs[4]
    came = lax.rem(spot()[2] + 4 - root_of(start)[1], 4)
    for d, piece in enumerate(pieces):

        @pl.when(came == d)
        def _():
            out[...] = piece[...]


def unit_rows_kernel(start, here, there, piece):
    is_here = root_of(start)[2] == lax.axis_index("zl")
    wide = jnp.where(is_here, here[...].astype(F32), there[...].astype(F32))
    total = jnp.sum(wide * wide, axis=1, keepdims=True)
    piece[...] = (wide * lax.rsqrt(total + EPSILON)).astype(BF16)


def gather_kernel(*refs):
    chunk = refs[4]
    place = spot()[2]
    for d in range(4):
        chunk[window(back(place, d), PIECE), :] = refs[d][...]


def unit_columns_kernel(own, one, three, two_low, two_high, out):
    mine = lax.axis_index("t")
    total = [jnp.zeros((1, HALF), F32)] * 2
    parts = []
    for d, low, high in ((0, own, own), (1, one, one), (3, three, three), (2, two_low, two_high)):
        for side, piece in enumerate((low, high)):
            at = side * HALF if piece.shape[1] == ROWS else 0
            parts.append((d, side, piece, at))
            wide = piece[:, at : at + HALF].astype(F32)
            total[side] = total[side] + jnp.sum(wide * wide, axis=0, keepdims=True)
    scale = [lax.rsqrt(value + EPSILON) for value in total]
    for d, side, piece, at in parts:
        wide = piece[:, at : at + HALF].astype(F32)
        out[window(back(mine, d), PART), side * HALF : side * HALF + HALF] = (wide * scale[side]).astype(BF16)


def slab_weights(other, start, multiplier, offset, chunks, images, text, weights):
    place = spot()[1 + other]
    held = lax.axis_index(DP) == holder_of(start, other)[1]
    times, plus = multiplier[0], offset[0]
    for d in range(4):
        rows = slice(CHUNK * d, CHUNK * d + CHUNK)
        text[rows, :] = chunks[d][...]
        logits = times * jnp.dot(chunks[d][...], images[...], preferred_element_type=F32) + plus
        row = lax.broadcasted_iota(jnp.int32, (CHUNK, 1), 0) + back(place, d) * CHUNK
        same = row == lax.broadcasted_iota(jnp.int32, (CHUNK, ROWS), 1)
        positive = jnp.where(same & held, 1.0, 0.0)
        share = 0.5 * jnp.tanh(0.5 * logits) + 0.5
        weights[rows, :] = ((share - positive) * times).astype(BF16)


def slab_terms(other, images, weights, by_owner, keep, send):
    core, place = lax.axis_index("c"), spot()[1 + other]
    for d in range(4):
        terms = lax.dot_general(
            weights[CHUNK * d : CHUNK * d + CHUNK, :],
            images[...],
            (((1,), (1,)), ((), ())),
            preferred_element_type=F32,
        )
        for inner in range(4):
            x, z = back(place, d), inner >> 1
            for low in range(2):
                y = (inner & 1) * 2 + low
                spots = (x * 4 + y, y * 4 + x)
                for c in range(2):
                    at = PIECE * inner + 16 * low + 8 * c
                    by_owner[c, spots[c], 8 * z : 8 * z + 8, :] = terms[at : at + 8, :]
    keep[...] = by_owner[core]
    send[...] = by_owner[1 - core].astype(BF16)


def turned_product(text, weights):
    return lax.dot_general(text[...], weights[...], (((0,), (0,)), ((), ())), preferred_element_type=F32)


def own_kernel(start, multiplier, offset, *refs):
    chunks, (images, keep, send, grad, text, weights, by_owner) = refs[:4], refs[4:]
    slab_weights(0, start, multiplier, offset, chunks, images, text, weights)
    slab_terms(0, images, weights, by_owner, keep, send)
    grad[...] = turned_product(text, weights)


def other_kernel(start, multiplier, offset, *refs):
    chunks, (images, keep, send, weights, text, by_owner) = refs[:4], refs[4:]
    slab_weights(1, start, multiplier, offset, chunks, images, text, weights)
    slab_terms(1, images, weights, by_owner, keep, send)


def pieces_kernel(*refs):
    chunks, (weights, before), pieces, (text, grad) = refs[:4], refs[4:6], refs[6:10], refs[10:]
    for d in range(4):
        text[CHUNK * d : CHUNK * d + CHUNK, :] = chunks[d][...]
    mine = lax.axis_index("t")
    grad[...] = before[...] + turned_product(text, weights)
    for d, piece in enumerate(pieces):
        piece[...] = grad[window(ahead(mine, d), PART), :].astype(BF16)


def join_kernel(own, from_other, other, from_own, *outs):
    place = spot()[1]
    for d, out in enumerate(outs):
        rows = window(ahead(place, d), 4)
        out[:, :16, :] = (own[rows] + from_other[rows].astype(F32)).astype(out.dtype)
        out[:, 16:, :] = (other[rows] + from_own[rows].astype(F32)).astype(out.dtype)


def first_sum_kernel(own, one, two, three, *refs):
    outs, total = refs[:4], refs[4]
    place = spot()[2]
    total[...] = (own[...] + one[...].astype(F32)) + (two[...].astype(F32) + three[...].astype(F32))
    for d, out in enumerate(outs):
        out[...] = total[ahead(place, d)].astype(out.dtype)


def second_sum_kernel(start, own, one, two, three, keep, send, total):
    z_lo = lax.axis_index("zl")
    step = holder_of(start, 0)[0]
    total[...] = (own[...] + one[...].astype(F32)) + (two[...].astype(F32) + three[...].astype(F32))
    for slab, at in ((0, step), (1, 1 - step)):
        keep[at] = total[window(2 * slab + z_lo, 8), :]
        send[at] = total[window(2 * slab + 1 - z_lo, 8), :]


def lay_copies(places, out, done):
    mine = lax.axis_index("t")
    run(
        [
            pltpu.make_async_copy(piece, out.at[:, window(back(mine, d), ROWS)], done.at[i])
            for i, (d, piece) in enumerate(places)
        ]
    )


def lay_near_kernel(own, one, three, out, done):
    lay_copies([(0, own), (1, one), (3, three)], out, done)


def lay_far_kernel(two, before, out, done):
    lay_copies([(2, two)], out, done)


def lay_near(own, one, three):
    return pl.pallas_call(
        lay_near_kernel,
        out_shape=like(PART, PEERS * ROWS),
        in_specs=[VMEM] * 3,
        out_specs=HBM,
        compiler_params=pltpu.CompilerParams(vmem_limit_bytes=4 << 20),
        scratch_shapes=[DMA((3,))],
    )(own, one, three)


def lay_far(two, before):
    return pl.pallas_call(
        lay_far_kernel,
        out_shape=like(PART, PEERS * ROWS),
        in_specs=[VMEM, HBM],
        out_specs=HBM,
        compiler_params=pltpu.CompilerParams(vmem_limit_bytes=4 << 20),
        scratch_shapes=[DMA((1,))],
        input_output_aliases={1: 0},
    )(two, before)


def per_device(pictures, captions, start, multiplier, offset):
    start, multiplier, offset = (value.reshape(1) for value in (start, multiplier, offset))
    scalars, scalar_specs = (start, multiplier, offset), [SMEM] * 3

    pictures = pictures.T
    *chunks, near, one, three = call(
        cut_kernel,
        [like(4, PIECE, D)] * 4 + [like(PART, ROWS)] * 3,
        [HBM] * 2,
        [DMA((4,)), DMA((3,))],
        moved=4,
        vmem=58 << 20,
    )(captions.reshape(4, 4, PIECE, D), pictures)

    chunks = [chunks[0]] + [along(chunks[d], True, d) for d in (1, 2, 3)]
    one, three = shift(one, "t", 1, PEERS), shift(three, "t", 3, PEERS)
    pieces = call(first_pick_kernel, [like(PIECE, D)] * 4, [SMEM] + [VMEM] * 4)(start, *chunks)
    pieces = [pieces[0]] + [along(pieces[d], False, d) for d in (1, 2, 3)]
    piece = call(second_pick_kernel, like(PIECE, D), [SMEM] + [VMEM] * 4)(start, *pieces)
    there = shift(piece, "zl", 1, 2)
    there, one, three = lax.optimization_barrier((there, one, three))
    low, high = call(cut_far_kernel, [like(PART, HALF)] * 2, [HBM], [DMA((2,))])(pictures)
    low, high = shift(low, "t", 2, PEERS), shift(high, "t", 2, PEERS)
    piece = call(unit_rows_kernel, like(PIECE, D), [SMEM] + [VMEM] * 2)(start, piece, there)

    pieces = [piece] + [along(piece, False, d) for d in (1, 2, 3)]
    *pieces, low = lax.optimization_barrier((*pieces, low))
    chunk = call(gather_kernel, like(CHUNK, D), [VMEM] * 4)(*pieces)
    own = [chunk] + [along(chunk, True, d) for d in (1, 2, 3)]
    *own, high = lax.optimization_barrier((*own, high))
    theirs = [shift(chunk, "c", 1, 2) for chunk in own]
    images = call(unit_columns_kernel, like(D, ROWS), [VMEM] * 5, moved=3)(near, one, three, low, high)

    text_scratch, owner_scratch = pltpu.VMEM((ROWS, D), BF16), pltpu.VMEM((2,) + OWNED, F32)
    kept, sent, square = like(*OWNED, dtype=F32), like(*OWNED), like(ROWS, ROWS)
    keep_own, send_own, grad = call(
        own_kernel,
        [kept, sent, like(D, ROWS, dtype=F32)],
        scalar_specs + [VMEM] * 5,
        [text_scratch, pltpu.VMEM((ROWS, ROWS), BF16), owner_scratch],
        products=3,
        moved=8,
    )(*scalars, *own, images)
    keep_other, send_other, weights = call(
        other_kernel,
        [kept, sent, square],
        scalar_specs + [VMEM] * 5,
        [text_scratch, owner_scratch],
        products=2,
        moved=5,
    )(*scalars, *theirs, images)
    pieces = call(
        pieces_kernel,
        [like(PART, ROWS)] * PEERS,
        [VMEM] * 6,
        [text_scratch, pltpu.VMEM((D, ROWS), F32)],
        products=1,
        moved=5,
    )(*theirs, weights, grad)
    *pieces, keep_own = lax.optimization_barrier((*pieces, keep_own))
    returned = [pieces[0]] + [shift(pieces[d], "t", d, PEERS) for d in (1, 2, 3)]

    parts = call(
        join_kernel, [like(4, PIECE, D, dtype=F32)] + [like(4, PIECE, D)] * 3, [VMEM] * 4, moved=4
    )(keep_own, shift(send_other, "c", 1, 2), keep_other, shift(send_own, "c", 1, 2))
    parts = [parts[0]] + [along(parts[d], True, d) for d in (1, 2, 3)]
    *parts, returned[1], returned[3] = lax.optimization_barrier((*parts, returned[1], returned[3]))
    parts = call(
        first_sum_kernel,
        [like(PIECE, D, dtype=F32)] + [like(PIECE, D)] * 3,
        [VMEM] * 4,
        [pltpu.VMEM((4, PIECE, D), F32)],
    )(*parts)
    parts = [parts[0]] + [along(parts[d], False, d) for d in (1, 2, 3)]
    keep, send = call(
        second_sum_kernel, [like(2, 8, D, dtype=F32)] * 2, [SMEM] + [VMEM] * 4, [pltpu.VMEM((PIECE, D), F32)]
    )(start, *parts)
    text_grad = keep + shift(send, "zl", 1, 2)
    image_grad = lay_far(returned[2], lay_near(returned[0], returned[1], returned[3]))
    return image_grad.T, text_grad[:, None]


def solution(mesh):
    names, sizes = zip(*SIZES)
    grid = Mesh(mesh.devices.reshape(sizes), names)
    return jax.shard_map(
        per_device,
        mesh=grid,
        in_specs=(P(DP, "t"), P(names, None), P(), P(), P()),
        out_specs=(P(DP, "t"), P(None, "t", DP, None)),
        check_vma=False,
    )
```

```python
import jax
import jax.numpy as jnp
from jax import lax
from jax.experimental import pallas as pl
from jax.experimental.pallas import tpu as pltpu
from jax.sharding import Mesh
from jax.sharding import PartitionSpec as P

EPSILON = 1e-06
SIZES = (("x", 4), ("zl", 2), ("y", 4), ("c", 2), ("t", 4))
DP = ("x", "zl", "y", "c")
D, ROWS, PART, PEERS = 1152, 512, 288, 4
CHUNK, PIECE, HALF = 128, 32, 256
OWNED = (16, 16, D)
F32, BF16 = jnp.float32, jnp.bfloat16
VMEM, SMEM, HBM = (pl.BlockSpec(memory_space=space) for space in (pltpu.VMEM, pltpu.SMEM, pltpu.HBM))
DMA = pltpu.SemaphoreType.DMA


def like(*shape, dtype=BF16):
    return jax.ShapeDtypeStruct(shape, dtype)


def call(kernel, outs, ins, scratch=(), products=0, moved=1, vmem=16 << 20):
    single = not isinstance(outs, list)
    return pl.pallas_call(
        kernel,
        out_shape=outs,
        in_specs=ins,
        out_specs=VMEM if single else [VMEM] * len(outs),
        scratch_shapes=list(scratch),
        compiler_params=pltpu.CompilerParams(vmem_limit_bytes=vmem),
        cost_estimate=pl.CostEstimate(
            flops=2 * products * D * ROWS * ROWS, bytes_accessed=moved << 20, transcendentals=0
        ),
    )


def shift(value, axis, by, size):
    return lax.ppermute(value, axis, [(i, (i + by) % size) for i in range(size)])


def along(value, first, by):
    pairs = []
    for i in range(64):
        x, z, y, c = i >> 4, (i >> 3) & 1, (i >> 1) & 3, i & 1
        if (c == 0) == first:
            x = (x + by) % 4
        else:
            y = (y + by) % 4
        pairs.append((i, ((x * 2 + z) * 4 + y) * 2 + c))
    return lax.ppermute(value, DP, pairs)


def spot():
    x, y, c = lax.axis_index("x"), lax.axis_index("y"), lax.axis_index("c")
    return c, jnp.where(c == 0, x, y), jnp.where(c == 0, y, x)


def holder_of(start, other):
    step = (start[0] + lax.axis_index("c") + other) & 1
    return step, lax.rem(start[0] + step, 64)


def back(place, d):
    return lax.rem(place + (4 - d), 4)


def ahead(place, d):
    return lax.rem(place + d, 4)


def window(index, size):
    return pl.ds(pl.multiple_of(index * size, size), size)


def run(copies):
    for copy in copies:
        copy.start()
    for copy in copies:
        copy.wait()


def cut_pieces(places, pictures, done):
    mine = lax.axis_index("t")
    copies = []
    for i, (piece, d, at) in enumerate(places):
        size = piece.shape[1]
        rows = pl.ds(pl.multiple_of(ahead(mine, d) * ROWS + at, HALF), size)
        copies.append(pltpu.make_async_copy(pictures.at[:, rows], piece, done.at[i]))
    run(copies)


def cut_text_kernel(captions, *refs):
    chunks, done = refs[:4], refs[4]
    place = spot()[1]
    run(
        [
            pltpu.make_async_copy(captions.at[ahead(place, d)], chunk, done.at[d])
            for d, chunk in enumerate(chunks)
        ]
    )


def cut_near_kernel(pictures, own, one, three, done):
    cut_pieces([(own, 0, 0), (one, 1, 0), (three, 3, 0)], pictures, done)


def cut_far_kernel(pictures, low, high, done):
    cut_pieces([(low, 2, 0), (high, 2, HALF)], pictures, done)


def root_of(start):
    chip = holder_of(start, 0)[1] >> 1
    x, y, core = chip >> 3, chip & 3, lax.axis_index("c")
    return jnp.where(core == 0, x, y), jnp.where(core == 0, y, x), (chip >> 2) & 1


def first_pick_kernel(start, *refs):
    chunks, outs = refs[:4], refs[4:]
    _, first, second = spot()
    came = lax.rem(first + 4 - root_of(start)[0], 4)
    for d, chunk in enumerate(chunks):

        @pl.when(came == d)
        def _():
            for by, out in enumerate(outs):
                out[...] = chunk[ahead(second, by)]


def second_pick_kernel(start, *refs):
    pieces, out = refs[:4], refs[4]
    came = lax.rem(spot()[2] + 4 - root_of(start)[1], 4)
    for d, piece in enumerate(pieces):

        @pl.when(came == d)
        def _():
            out[...] = piece[...]


def unit_rows_kernel(start, here, there, piece):
    is_here = root_of(start)[2] == lax.axis_index("zl")
    wide = jnp.where(is_here, here[...].astype(F32), there[...].astype(F32))
    total = jnp.sum(wide * wide, axis=1, keepdims=True)
    piece[...] = (wide * lax.rsqrt(total + EPSILON)).astype(BF16)


def gather_kernel(*refs):
    chunk = refs[4]
    place = spot()[2]
    for d in range(4):
        chunk[window(back(place, d), PIECE), :] = refs[d][...]


def unit_columns_kernel(own, one, three, two_low, two_high, out):
    mine = lax.axis_index("t")
    total = [jnp.zeros((1, HALF), F32)] * 2
    parts = []
    for d, low, high in ((0, own, own), (1, one, one), (3, three, three), (2, two_low, two_high)):
        for side, piece in enumerate((low, high)):
            at = side * HALF if piece.shape[1] == ROWS else 0
            parts.append((d, side, piece, at))
            wide = piece[:, at : at + HALF].astype(F32)
            total[side] = total[side] + jnp.sum(wide * wide, axis=0, keepdims=True)
    scale = [lax.rsqrt(value + EPSILON) for value in total]
    for d, side, piece, at in parts:
        wide = piece[:, at : at + HALF].astype(F32)
        out[window(back(mine, d), PART), side * HALF : side * HALF + HALF] = (wide * scale[side]).astype(BF16)


def slab_weights(other, start, multiplier, offset, chunks, images, text, weights):
    place = spot()[1 + other]
    held = lax.axis_index(DP) == holder_of(start, other)[1]
    times, plus = multiplier[0], offset[0]
    for d in range(4):
        rows = slice(CHUNK * d, CHUNK * d + CHUNK)
        text[rows, :] = chunks[d][...]
        logits = times * jnp.dot(chunks[d][...], images[...], preferred_element_type=F32) + plus
        row = lax.broadcasted_iota(jnp.int32, (CHUNK, 1), 0) + back(place, d) * CHUNK
        same = row == lax.broadcasted_iota(jnp.int32, (CHUNK, ROWS), 1)
        positive = jnp.where(same & held, 1.0, 0.0)
        share = 0.5 * jnp.tanh(0.5 * logits) + 0.5
        weights[rows, :] = ((share - positive) * times).astype(BF16)


def slab_terms(other, images, weights, keep, send):
    core, x = lax.axis_index("c"), spot()[1 + other]
    for d in range(4):
        terms = lax.dot_general(
            weights[CHUNK * d : CHUNK * d + CHUNK, :],
            images[...],
            (((1,), (1,)), ((), ())),
            preferred_element_type=F32,
        )
        outer = back(x, d)
        for y in range(4):
            rows = []
            for c in range(2):
                at = 16 * y + 8 * c
                rows.append(jnp.concatenate([terms[at : at + 8, :], terms[at + 64 : at + 72, :]]))
            straight, turned = outer * 4 + y, y * 4 + outer
            kept, sent = (jnp.where(core == 0, *pair) for pair in (rows, rows[::-1]))
            keep[jnp.where(core == 0, straight, turned)] = kept
            send[jnp.where(core == 0, turned, straight)] = sent.astype(BF16)


def turned_product(text, weights):
    return lax.dot_general(text[...], weights[...], (((0,), (0,)), ((), ())), preferred_element_type=F32)


def own_kernel(start, multiplier, offset, *refs):
    chunks, (images, keep, send, grad, text, weights) = refs[:4], refs[4:]
    slab_weights(0, start, multiplier, offset, chunks, images, text, weights)
    slab_terms(0, images, weights, keep, send)
    grad[...] = turned_product(text, weights)


def other_kernel(start, multiplier, offset, *refs):
    chunks, (images, keep, send, weights, text) = refs[:4], refs[4:]
    slab_weights(1, start, multiplier, offset, chunks, images, text, weights)
    slab_terms(1, images, weights, keep, send)


def pieces_kernel(*refs):
    chunks, (weights, before), pieces, (text, grad) = refs[:4], refs[4:6], refs[6:10], refs[10:]
    for d in range(4):
        text[CHUNK * d : CHUNK * d + CHUNK, :] = chunks[d][...]
    mine = lax.axis_index("t")
    grad[...] = before[...] + turned_product(text, weights)
    for d, piece in enumerate(pieces):
        piece[...] = grad[window(ahead(mine, d), PART), :].astype(BF16)


def join_kernel(own, from_other, other, from_own, *outs):
    place = spot()[1]
    for d, out in enumerate(outs):
        rows = window(ahead(place, d), 4)
        out[:, :16, :] = (own[rows] + from_other[rows].astype(F32)).astype(out.dtype)
        out[:, 16:, :] = (other[rows] + from_own[rows].astype(F32)).astype(out.dtype)


def first_sum_kernel(own, one, two, three, *refs):
    outs, total = refs[:4], refs[4]
    place = spot()[2]
    total[...] = (own[...] + one[...].astype(F32)) + (two[...].astype(F32) + three[...].astype(F32))
    for d, out in enumerate(outs):
        out[...] = total[ahead(place, d)].astype(out.dtype)


def second_sum_kernel(start, own, one, two, three, keep, send, total):
    z_lo = lax.axis_index("zl")
    step = holder_of(start, 0)[0]
    total[...] = (own[...] + one[...].astype(F32)) + (two[...].astype(F32) + three[...].astype(F32))
    for slab, at in ((0, step), (1, 1 - step)):
        keep[at] = total[window(2 * slab + z_lo, 8), :]
        send[at] = total[window(2 * slab + 1 - z_lo, 8), :].astype(BF16)


def lay_copies(places, out, done):
    mine = lax.axis_index("t")
    run(
        [
            pltpu.make_async_copy(piece, out.at[:, window(back(mine, d), ROWS)], done.at[i])
            for i, (d, piece) in enumerate(places)
        ]
    )


def lay_near_kernel(own, one, three, out, done):
    lay_copies([(0, own), (1, one), (3, three)], out, done)


def lay_far_kernel(two, before, out, done):
    lay_copies([(2, two)], out, done)


def lay_near(own, one, three):
    return pl.pallas_call(
        lay_near_kernel,
        out_shape=like(PART, PEERS * ROWS),
        in_specs=[VMEM] * 3,
        out_specs=HBM,
        compiler_params=pltpu.CompilerParams(vmem_limit_bytes=4 << 20),
        scratch_shapes=[DMA((3,))],
    )(own, one, three)


def lay_far(two, before):
    return pl.pallas_call(
        lay_far_kernel,
        out_shape=like(PART, PEERS * ROWS),
        in_specs=[VMEM, HBM],
        out_specs=HBM,
        compiler_params=pltpu.CompilerParams(vmem_limit_bytes=4 << 20),
        scratch_shapes=[DMA((1,))],
        input_output_aliases={1: 0},
    )(two, before)


def per_device(pictures, captions, start, multiplier, offset):
    start, multiplier, offset = (value.reshape(1) for value in (start, multiplier, offset))
    scalars, scalar_specs = (start, multiplier, offset), [SMEM] * 3

    pictures = pictures.T
    near, one, three = call(cut_near_kernel, [like(PART, ROWS)] * 3, [HBM], [DMA((3,))], moved=2)(pictures)

    chunks = call(cut_text_kernel, [like(4, PIECE, D)] * 4, [HBM], [DMA((4,))], moved=2, vmem=60 << 20)(
        captions.reshape(4, 4, PIECE, D)
    )
    chunks = [chunks[0]] + [along(chunks[d], True, d) for d in (1, 2, 3)]
    one, three = shift(one, "t", 1, PEERS), shift(three, "t", 3, PEERS)
    pieces = call(first_pick_kernel, [like(PIECE, D)] * 4, [SMEM] + [VMEM] * 4)(start, *chunks)
    pieces = [pieces[0]] + [along(pieces[d], False, d) for d in (1, 2, 3)]
    piece = call(second_pick_kernel, like(PIECE, D), [SMEM] + [VMEM] * 4)(start, *pieces)
    there = shift(piece, "zl", 1, 2)
    there, one, three = lax.optimization_barrier((there, one, three))
    low, high = call(cut_far_kernel, [like(PART, HALF)] * 2, [HBM], [DMA((2,))])(pictures)
    low, high = shift(low, "t", 2, PEERS), shift(high, "t", 2, PEERS)
    piece = call(unit_rows_kernel, like(PIECE, D), [SMEM] + [VMEM] * 2)(start, piece, there)

    pieces = [piece] + [along(piece, False, d) for d in (1, 2, 3)]
    *pieces, low = lax.optimization_barrier((*pieces, low))
    chunk = call(gather_kernel, like(CHUNK, D), [VMEM] * 4)(*pieces)
    own = [chunk] + [along(chunk, True, d) for d in (1, 2, 3)]
    *own, high = lax.optimization_barrier((*own, high))
    theirs = [shift(chunk, "c", 1, 2) for chunk in own]
    images = call(unit_columns_kernel, like(D, ROWS), [VMEM] * 5, moved=3)(near, one, three, low, high)

    text_scratch = pltpu.VMEM((ROWS, D), BF16)
    kept, sent, square = like(*OWNED, dtype=F32), like(*OWNED), like(ROWS, ROWS)
    keep_own, send_own, grad = call(
        own_kernel,
        [kept, sent, like(D, ROWS, dtype=F32)],
        scalar_specs + [VMEM] * 5,
        [text_scratch, pltpu.VMEM((ROWS, ROWS), BF16)],
        products=3,
        moved=8,
    )(*scalars, *own, images)
    keep_other, send_other, weights = call(
        other_kernel,
        [kept, sent, square],
        scalar_specs + [VMEM] * 5,
        [text_scratch],
        products=2,
        moved=5,
    )(*scalars, *theirs, images)
    pieces = call(
        pieces_kernel,
        [like(PART, ROWS)] * PEERS,
        [VMEM] * 6,
        [text_scratch, pltpu.VMEM((D, ROWS), F32)],
        products=1,
        moved=5,
    )(*theirs, weights, grad)
    *pieces, keep_own = lax.optimization_barrier((*pieces, keep_own))
    returned = [pieces[0]] + [shift(pieces[d], "t", d, PEERS) for d in (1, 2, 3)]

    parts = call(
        join_kernel, [like(4, PIECE, D, dtype=F32)] + [like(4, PIECE, D)] * 3, [VMEM] * 4, moved=4
    )(keep_own, shift(send_other, "c", 1, 2), keep_other, shift(send_own, "c", 1, 2))
    parts = [parts[0]] + [along(parts[d], True, d) for d in (1, 2, 3)]
    parts = call(
        first_sum_kernel,
        [like(PIECE, D, dtype=F32)] + [like(PIECE, D)] * 3,
        [VMEM] * 4,
        [pltpu.VMEM((4, PIECE, D), F32)],
    )(*parts)
    parts = [parts[0]] + [along(parts[d], False, d) for d in (1, 2, 3)]
    keep, send = call(
        second_sum_kernel, [like(2, 8, D, dtype=F32), like(2, 8, D)], [SMEM] + [VMEM] * 4, [pltpu.VMEM((PIECE, D), F32)]
    )(start, *parts)
    text_grad = keep + shift(send, "zl", 1, 2).astype(F32)
    image_grad = lay_far(returned[2], lay_near(returned[0], returned[1], returned[3]))
    return image_grad.T, text_grad[:, None]


def solution(mesh):
    names, sizes = zip(*SIZES)
    grid = Mesh(mesh.devices.reshape(sizes), names)
    return jax.shard_map(
        per_device,
        mesh=grid,
        in_specs=(P(DP, "t"), P(names, None), P(), P(), P()),
        out_specs=(P(DP, "t"), P(None, "t", DP, None)),
        check_vma=False,
    )
```

```python
import jax
import jax.numpy as jnp
from jax import lax
from jax.experimental import pallas as pl
from jax.experimental.pallas import tpu as pltpu
from jax.sharding import Mesh
from jax.sharding import PartitionSpec as P

EPSILON = 1e-06
SIZES = (("x", 4), ("zl", 2), ("y", 4), ("c", 2), ("t", 4))
DP = ("x", "zl", "y", "c")
D, ROWS, PART, PEERS = 1152, 512, 288, 4
CHUNK, PIECE, HALF = 128, 32, 256
OWNED = (16, 16, D)
F32, BF16 = jnp.float32, jnp.bfloat16
VMEM, SMEM, HBM = (pl.BlockSpec(memory_space=space) for space in (pltpu.VMEM, pltpu.SMEM, pltpu.HBM))
DMA = pltpu.SemaphoreType.DMA


def like(*shape, dtype=BF16):
    return jax.ShapeDtypeStruct(shape, dtype)


def call(kernel, outs, ins, scratch=(), products=0, moved=1, vmem=12 << 20):
    single = not isinstance(outs, list)
    return pl.pallas_call(
        kernel,
        out_shape=outs,
        in_specs=ins,
        out_specs=VMEM if single else [VMEM] * len(outs),
        scratch_shapes=list(scratch),
        compiler_params=pltpu.CompilerParams(vmem_limit_bytes=vmem),
        cost_estimate=pl.CostEstimate(
            flops=2 * products * D * ROWS * ROWS, bytes_accessed=moved << 20, transcendentals=0
        ),
    )


def shift(value, axis, by, size):
    return lax.ppermute(value, axis, [(i, (i + by) % size) for i in range(size)])


def along(value, first, by):
    pairs = []
    for i in range(64):
        x, z, y, c = i >> 4, (i >> 3) & 1, (i >> 1) & 3, i & 1
        if (c == 0) == first:
            x = (x + by) % 4
        else:
            y = (y + by) % 4
        pairs.append((i, ((x * 2 + z) * 4 + y) * 2 + c))
    return lax.ppermute(value, DP, pairs)


def spot():
    x, y, c = lax.axis_index("x"), lax.axis_index("y"), lax.axis_index("c")
    return c, jnp.where(c == 0, x, y), jnp.where(c == 0, y, x)


def holder_of(start, other):
    step = (start[0] + lax.axis_index("c") + other) & 1
    return step, lax.rem(start[0] + step, 64)


def back(place, d):
    return lax.rem(place + (4 - d), 4)


def ahead(place, d):
    return lax.rem(place + d, 4)


def window(index, size):
    return pl.ds(pl.multiple_of(index * size, size), size)


def run(copies):
    for copy in copies:
        copy.start()
    for copy in copies:
        copy.wait()


def cut_pieces(places, pictures, done):
    mine = lax.axis_index("t")
    copies = []
    for i, (piece, d, at) in enumerate(places):
        size = piece.shape[1]
        rows = pl.ds(pl.multiple_of(ahead(mine, d) * ROWS + at, HALF), size)
        copies.append(pltpu.make_async_copy(pictures.at[:, rows], piece, done.at[i]))
    run(copies)


def cut_text_kernel(captions, *refs):
    chunks, done = refs[:4], refs[4]
    place = spot()[1]
    run(
        [
            pltpu.make_async_copy(captions.at[ahead(place, d)], chunk, done.at[d])
            for d, chunk in enumerate(chunks)
        ]
    )


def cut_near_kernel(pictures, own, one, three, done):
    cut_pieces([(own, 0, 0), (one, 1, 0), (three, 3, 0)], pictures, done)


def cut_far_kernel(pictures, low, high, done):
    cut_pieces([(low, 2, 0), (high, 2, HALF)], pictures, done)


def root_of(start):
    chip = holder_of(start, 0)[1] >> 1
    x, y, core = chip >> 3, chip & 3, lax.axis_index("c")
    return jnp.where(core == 0, x, y), jnp.where(core == 0, y, x), (chip >> 2) & 1


def first_pick_kernel(start, *refs):
    chunks, outs = refs[:4], refs[4:]
    _, first, second = spot()
    came = lax.rem(first + 4 - root_of(start)[0], 4)
    for d, chunk in enumerate(chunks):

        @pl.when(came == d)
        def _():
            for by, out in enumerate(outs):
                out[...] = chunk[ahead(second, by)]


def second_pick_kernel(start, *refs):
    pieces, out = refs[:4], refs[4]
    came = lax.rem(spot()[2] + 4 - root_of(start)[1], 4)
    for d, piece in enumerate(pieces):

        @pl.when(came == d)
        def _():
            out[...] = piece[...]


def unit_rows_kernel(start, here, there, piece):
    is_here = root_of(start)[2] == lax.axis_index("zl")
    wide = jnp.where(is_here, here[...].astype(F32), there[...].astype(F32))
    total = jnp.sum(wide * wide, axis=1, keepdims=True)
    piece[...] = (wide * lax.rsqrt(total + EPSILON)).astype(BF16)


def gather_kernel(*refs):
    chunk = refs[4]
    place = spot()[2]
    for d in range(4):
        chunk[window(back(place, d), PIECE), :] = refs[d][...]


def unit_columns_kernel(own, one, three, two_low, two_high, out):
    mine = lax.axis_index("t")
    total = [jnp.zeros((1, HALF), F32)] * 2
    parts = []
    for d, low, high in ((0, own, own), (1, one, one), (3, three, three), (2, two_low, two_high)):
        for side, piece in enumerate((low, high)):
            at = side * HALF if piece.shape[1] == ROWS else 0
            parts.append((d, side, piece, at))
            wide = piece[:, at : at + HALF].astype(F32)
            total[side] = total[side] + jnp.sum(wide * wide, axis=0, keepdims=True)
    scale = [lax.rsqrt(value + EPSILON) for value in total]
    for d, side, piece, at in parts:
        wide = piece[:, at : at + HALF].astype(F32)
        out[window(back(mine, d), PART), side * HALF : side * HALF + HALF] = (wide * scale[side]).astype(BF16)


def slab_weights(other, start, multiplier, offset, chunks, images, text, weights):
    place = spot()[1 + other]
    held = lax.axis_index(DP) == holder_of(start, other)[1]
    times, plus = multiplier[0], offset[0]
    for d in range(4):
        rows = slice(CHUNK * d, CHUNK * d + CHUNK)
        text[rows, :] = chunks[d][...]
        logits = times * jnp.dot(chunks[d][...], images[...], preferred_element_type=F32) + plus
        row = lax.broadcasted_iota(jnp.int32, (CHUNK, 1), 0) + back(place, d) * CHUNK
        same = row == lax.broadcasted_iota(jnp.int32, (CHUNK, ROWS), 1)
        positive = jnp.where(same & held, 1.0, 0.0)
        share = 0.5 * jnp.tanh(0.5 * logits) + 0.5
        weights[rows, :] = ((share - positive) * times).astype(BF16)


def slab_terms(other, images, weights, keep, send):
    core, x = lax.axis_index("c"), spot()[1 + other]
    for d in range(4):
        terms = lax.dot_general(
            weights[CHUNK * d : CHUNK * d + CHUNK, :],
            images[...],
            (((1,), (1,)), ((), ())),
            preferred_element_type=F32,
        )
        outer = back(x, d)
        for y in range(4):
            rows = []
            for c in range(2):
                at = 16 * y + 8 * c
                rows.append(jnp.concatenate([terms[at : at + 8, :], terms[at + 64 : at + 72, :]]))
            straight, turned = outer * 4 + y, y * 4 + outer
            kept, sent = (jnp.where(core == 0, *pair) for pair in (rows, rows[::-1]))
            keep[jnp.where(core == 0, straight, turned)] = kept
            send[jnp.where(core == 0, turned, straight)] = sent.astype(BF16)


def turned_product(text, weights):
    return lax.dot_general(text[...], weights[...], (((0,), (0,)), ((), ())), preferred_element_type=F32)


def own_kernel(start, multiplier, offset, *refs):
    chunks, (images, keep, send, grad, text, weights) = refs[:4], refs[4:]
    slab_weights(0, start, multiplier, offset, chunks, images, text, weights)
    slab_terms(0, images, weights, keep, send)
    grad[...] = turned_product(text, weights)


def other_kernel(start, multiplier, offset, *refs):
    chunks, (images, keep, send, weights, text) = refs[:4], refs[4:]
    slab_weights(1, start, multiplier, offset, chunks, images, text, weights)
    slab_terms(1, images, weights, keep, send)


def pieces_kernel(*refs):
    chunks, (weights, before), pieces, (text, grad) = refs[:4], refs[4:6], refs[6:10], refs[10:]
    for d in range(4):
        text[CHUNK * d : CHUNK * d + CHUNK, :] = chunks[d][...]
    mine = lax.axis_index("t")
    grad[...] = before[...] + turned_product(text, weights)
    for d, piece in enumerate(pieces):
        piece[...] = grad[window(ahead(mine, d), PART), :].astype(BF16)


def join_kernel(own, from_other, other, from_own, *outs):
    place = spot()[1]
    for d, out in enumerate(outs):
        rows = window(ahead(place, d), 4)
        out[:, :16, :] = (own[rows] + from_other[rows].astype(F32)).astype(out.dtype)
        out[:, 16:, :] = (other[rows] + from_own[rows].astype(F32)).astype(out.dtype)


def first_sum_kernel(own, one, two, three, *refs):
    outs, total = refs[:4], refs[4]
    place = spot()[2]
    total[...] = (own[...] + one[...].astype(F32)) + (two[...].astype(F32) + three[...].astype(F32))
    for d, out in enumerate(outs):
        out[...] = total[ahead(place, d)].astype(out.dtype)


def second_sum_kernel(start, own, one, two, three, keep, send, total):
    z_lo = lax.axis_index("zl")
    step = holder_of(start, 0)[0]
    total[...] = (own[...] + one[...].astype(F32)) + (two[...].astype(F32) + three[...].astype(F32))
    for slab, at in ((0, step), (1, 1 - step)):
        keep[at] = total[window(2 * slab + z_lo, 8), :]
        send[at] = total[window(2 * slab + 1 - z_lo, 8), :].astype(BF16)


def lay_copies(places, out, done):
    mine = lax.axis_index("t")
    run(
        [
            pltpu.make_async_copy(piece, out.at[:, window(back(mine, d), ROWS)], done.at[i])
            for i, (d, piece) in enumerate(places)
        ]
    )


def lay_near_kernel(own, one, three, out, done):
    lay_copies([(0, own), (1, one), (3, three)], out, done)


def lay_far_kernel(two, before, out, done):
    lay_copies([(2, two)], out, done)


def lay_near(own, one, three):
    return pl.pallas_call(
        lay_near_kernel,
        out_shape=like(PART, PEERS * ROWS),
        in_specs=[VMEM] * 3,
        out_specs=HBM,
        compiler_params=pltpu.CompilerParams(vmem_limit_bytes=4 << 20),
        scratch_shapes=[DMA((3,))],
    )(own, one, three)


def lay_far(two, before):
    return pl.pallas_call(
        lay_far_kernel,
        out_shape=like(PART, PEERS * ROWS),
        in_specs=[VMEM, HBM],
        out_specs=HBM,
        compiler_params=pltpu.CompilerParams(vmem_limit_bytes=4 << 20),
        scratch_shapes=[DMA((1,))],
        input_output_aliases={1: 0},
    )(two, before)


def per_device(pictures, captions, start, multiplier, offset):
    start, multiplier, offset = (value.reshape(1) for value in (start, multiplier, offset))
    scalars, scalar_specs = (start, multiplier, offset), [SMEM] * 3

    pictures = pictures.T
    near, one, three = call(cut_near_kernel, [like(PART, ROWS)] * 3, [HBM], [DMA((3,))], moved=2)(pictures)

    chunks = call(cut_text_kernel, [like(4, PIECE, D)] * 4, [HBM], [DMA((4,))], moved=2, vmem=60 << 20)(
        captions.reshape(4, 4, PIECE, D)
    )
    chunks = [chunks[0]] + [along(chunks[d], True, d) for d in (1, 2, 3)]
    one, three = shift(one, "t", 1, PEERS), shift(three, "t", 3, PEERS)
    pieces = call(first_pick_kernel, [like(PIECE, D)] * 4, [SMEM] + [VMEM] * 4)(start, *chunks)
    pieces = [pieces[0]] + [along(pieces[d], False, d) for d in (1, 2, 3)]
    piece = call(second_pick_kernel, like(PIECE, D), [SMEM] + [VMEM] * 4)(start, *pieces)
    there = shift(piece, "zl", 1, 2)
    there, one, three = lax.optimization_barrier((there, one, three))
    low, high = call(cut_far_kernel, [like(PART, HALF)] * 2, [HBM], [DMA((2,))])(pictures)
    low, high = shift(low, "t", 2, PEERS), shift(high, "t", 2, PEERS)
    piece = call(unit_rows_kernel, like(PIECE, D), [SMEM] + [VMEM] * 2)(start, piece, there)

    pieces = [piece] + [along(piece, False, d) for d in (1, 2, 3)]
    *pieces, low = lax.optimization_barrier((*pieces, low))
    chunk = call(gather_kernel, like(CHUNK, D), [VMEM] * 4)(*pieces)
    own = [chunk] + [along(chunk, True, d) for d in (1, 2, 3)]
    theirs = [shift(chunk, "c", 1, 2) for chunk in own]
    images = call(unit_columns_kernel, like(D, ROWS), [VMEM] * 5, moved=3)(near, one, three, low, high)

    text_scratch = pltpu.VMEM((ROWS, D), BF16)
    kept, sent, square = like(*OWNED, dtype=F32), like(*OWNED), like(ROWS, ROWS)
    keep_own, send_own, grad = call(
        own_kernel,
        [kept, sent, like(D, ROWS, dtype=F32)],
        scalar_specs + [VMEM] * 5,
        [text_scratch, pltpu.VMEM((ROWS, ROWS), BF16)],
        products=3,
        moved=8,
    )(*scalars, *own, images)
    keep_other, send_other, weights = call(
        other_kernel,
        [kept, sent, square],
        scalar_specs + [VMEM] * 5,
        [text_scratch],
        products=2,
        moved=5,
    )(*scalars, *theirs, images)
    pieces = call(
        pieces_kernel,
        [like(PART, ROWS)] * PEERS,
        [VMEM] * 6,
        [text_scratch, pltpu.VMEM((D, ROWS), F32)],
        products=1,
        moved=5,
    )(*theirs, weights, grad)
    *pieces, keep_own = lax.optimization_barrier((*pieces, keep_own))
    returned = [pieces[0]] + [shift(pieces[d], "t", d, PEERS) for d in (1, 2, 3)]

    parts = call(
        join_kernel, [like(4, PIECE, D, dtype=F32)] + [like(4, PIECE, D)] * 3, [VMEM] * 4, moved=4
    )(keep_own, shift(send_other, "c", 1, 2), keep_other, shift(send_own, "c", 1, 2))
    parts = [parts[0]] + [along(parts[d], True, d) for d in (1, 2, 3)]
    parts = call(
        first_sum_kernel,
        [like(PIECE, D, dtype=F32)] + [like(PIECE, D)] * 3,
        [VMEM] * 4,
        [pltpu.VMEM((4, PIECE, D), F32)],
    )(*parts)
    parts = [parts[0]] + [along(parts[d], False, d) for d in (1, 2, 3)]
    keep, send = call(
        second_sum_kernel, [like(2, 8, D, dtype=F32), like(2, 8, D)], [SMEM] + [VMEM] * 4, [pltpu.VMEM((PIECE, D), F32)]
    )(start, *parts)
    text_grad = keep + shift(send, "zl", 1, 2).astype(F32)
    image_grad = lay_far(returned[2], lay_near(returned[0], returned[1], returned[3]))
    return image_grad.T, text_grad[:, None]


def solution(mesh):
    names, sizes = zip(*SIZES)
    grid = Mesh(mesh.devices.reshape(sizes), names)
    return jax.shard_map(
        per_device,
        mesh=grid,
        in_specs=(P(DP, "t"), P(names, None), P(), P(), P()),
        out_specs=(P(DP, "t"), P(None, "t", DP, None)),
        check_vma=False,
    )
```

```python
import jax
import jax.numpy as jnp
from jax import lax
from jax.experimental import pallas as pl
from jax.experimental.pallas import tpu as pltpu
from jax.sharding import Mesh
from jax.sharding import PartitionSpec as P

EPSILON = 1e-06
SIZES = (("x", 4), ("zl", 2), ("y", 4), ("c", 2), ("t", 4))
DP = ("x", "zl", "y", "c")
D, ROWS, PART, PEERS = 1152, 512, 288, 4
CHUNK, PIECE, HALF = 128, 32, 256
OWNED = (16, 16, D)
F32, BF16 = jnp.float32, jnp.bfloat16
VMEM, SMEM, HBM = (pl.BlockSpec(memory_space=space) for space in (pltpu.VMEM, pltpu.SMEM, pltpu.HBM))
DMA = pltpu.SemaphoreType.DMA


def like(*shape, dtype=BF16):
    return jax.ShapeDtypeStruct(shape, dtype)


def call(kernel, outs, ins, scratch=(), products=0, moved=1, vmem=12 << 20):
    single = not isinstance(outs, list)
    return pl.pallas_call(
        kernel,
        out_shape=outs,
        in_specs=ins,
        out_specs=VMEM if single else [VMEM] * len(outs),
        scratch_shapes=list(scratch),
        compiler_params=pltpu.CompilerParams(vmem_limit_bytes=vmem),
        cost_estimate=pl.CostEstimate(
            flops=2 * products * D * ROWS * ROWS, bytes_accessed=moved << 20, transcendentals=0
        ),
    )


def shift(value, axis, by, size):
    return lax.ppermute(value, axis, [(i, (i + by) % size) for i in range(size)])


def along(value, first, by):
    pairs = []
    for i in range(64):
        x, z, y, c = i >> 4, (i >> 3) & 1, (i >> 1) & 3, i & 1
        if (c == 0) == first:
            x = (x + by) % 4
        else:
            y = (y + by) % 4
        pairs.append((i, ((x * 2 + z) * 4 + y) * 2 + c))
    return lax.ppermute(value, DP, pairs)


def spot():
    x, y, c = lax.axis_index("x"), lax.axis_index("y"), lax.axis_index("c")
    return c, jnp.where(c == 0, x, y), jnp.where(c == 0, y, x)


def holder_of(start, other):
    step = (start[0] + lax.axis_index("c") + other) & 1
    return step, lax.rem(start[0] + step, 64)


def back(place, d):
    return lax.rem(place + (4 - d), 4)


def ahead(place, d):
    return lax.rem(place + d, 4)


def window(index, size):
    return pl.ds(pl.multiple_of(index * size, size), size)


def run(copies):
    for copy in copies:
        copy.start()
    for copy in copies:
        copy.wait()


def cut_pieces(places, pictures, done):
    mine = lax.axis_index("t")
    copies = []
    for i, (piece, d, at) in enumerate(places):
        size = piece.shape[1]
        rows = pl.ds(pl.multiple_of(ahead(mine, d) * ROWS + at, HALF), size)
        copies.append(pltpu.make_async_copy(pictures.at[:, rows], piece, done.at[i]))
    run(copies)


def cut_text_kernel(captions, *refs):
    chunks, done = refs[:4], refs[4]
    place = spot()[1]
    run(
        [
            pltpu.make_async_copy(captions.at[ahead(place, d)], chunk, done.at[d])
            for d, chunk in enumerate(chunks)
        ]
    )


def cut_near_kernel(pictures, own, one, three, done):
    cut_pieces([(own, 0, 0), (one, 1, 0), (three, 3, 0)], pictures, done)


def cut_far_kernel(pictures, low, high, done):
    cut_pieces([(low, 2, 0), (high, 2, HALF)], pictures, done)


def root_of(start):
    chip = holder_of(start, 0)[1] >> 1
    x, y, core = chip >> 3, chip & 3, lax.axis_index("c")
    return jnp.where(core == 0, x, y), jnp.where(core == 0, y, x), (chip >> 2) & 1


def first_pick_kernel(start, *refs):
    chunks, outs = refs[:4], refs[4:]
    _, first, second = spot()
    came = lax.rem(first + 4 - root_of(start)[0], 4)
    for d, chunk in enumerate(chunks):

        @pl.when(came == d)
        def _():
            for by, out in enumerate(outs):
                out[...] = chunk[ahead(second, by)]


def second_pick_kernel(start, *refs):
    pieces, out = refs[:4], refs[4]
    came = lax.rem(spot()[2] + 4 - root_of(start)[1], 4)
    for d, piece in enumerate(pieces):

        @pl.when(came == d)
        def _():
            out[...] = piece[...]


def unit_rows_kernel(start, here, there, piece):
    is_here = root_of(start)[2] == lax.axis_index("zl")
    wide = jnp.where(is_here, here[...].astype(F32), there[...].astype(F32))
    total = jnp.sum(wide * wide, axis=1, keepdims=True)
    piece[...] = (wide * lax.rsqrt(total + EPSILON)).astype(BF16)


def gather_kernel(*refs):
    chunk = refs[4]
    place = spot()[2]
    for d in range(4):
        chunk[window(back(place, d), PIECE), :] = refs[d][...]


def unit_columns_kernel(own, one, three, two_low, two_high, out):
    mine = lax.axis_index("t")
    total = [jnp.zeros((1, HALF), F32)] * 2
    parts = []
    for d, low, high in ((0, own, own), (1, one, one), (3, three, three), (2, two_low, two_high)):
        for side, piece in enumerate((low, high)):
            at = side * HALF if piece.shape[1] == ROWS else 0
            parts.append((d, side, piece, at))
            wide = piece[:, at : at + HALF].astype(F32)
            total[side] = total[side] + jnp.sum(wide * wide, axis=0, keepdims=True)
    scale = [lax.rsqrt(value + EPSILON) for value in total]
    for d, side, piece, at in parts:
        wide = piece[:, at : at + HALF].astype(F32)
        out[window(back(mine, d), PART), side * HALF : side * HALF + HALF] = (wide * scale[side]).astype(BF16)


def slab_weights(other, start, multiplier, offset, chunks, images, text, weights):
    place = spot()[1 + other]
    held = lax.axis_index(DP) == holder_of(start, other)[1]
    times, plus = multiplier[0], offset[0]
    for d in range(4):
        rows = slice(CHUNK * d, CHUNK * d + CHUNK)
        text[rows, :] = chunks[d][...]
        logits = times * jnp.dot(chunks[d][...], images[...], preferred_element_type=F32) + plus
        row = lax.broadcasted_iota(jnp.int32, (CHUNK, 1), 0) + back(place, d) * CHUNK
        same = row == lax.broadcasted_iota(jnp.int32, (CHUNK, ROWS), 1)
        positive = jnp.where(same & held, 1.0, 0.0)
        share = 0.5 * jnp.tanh(0.5 * logits) + 0.5
        weights[rows, :] = ((share - positive) * times).astype(BF16)


def slab_terms(other, images, weights, keep, send):
    core, x = lax.axis_index("c"), spot()[1 + other]
    for d in range(4):
        terms = lax.dot_general(
            weights[CHUNK * d : CHUNK * d + CHUNK, :],
            images[...],
            (((1,), (1,)), ((), ())),
            preferred_element_type=F32,
        )
        outer = back(x, d)
        for y in range(4):
            rows = []
            for c in range(2):
                at = 16 * y + 8 * c
                rows.append(jnp.concatenate([terms[at : at + 8, :], terms[at + 64 : at + 72, :]]))
            straight, turned = outer * 4 + y, y * 4 + outer
            kept, sent = (jnp.where(core == 0, *pair) for pair in (rows, rows[::-1]))
            keep[jnp.where(core == 0, straight, turned)] = kept
            send[jnp.where(core == 0, turned, straight)] = sent.astype(BF16)


def turned_product(text, weights):
    return lax.dot_general(text[...], weights[...], (((0,), (0,)), ((), ())), preferred_element_type=F32)


def terms_kernel(other, start, multiplier, offset, *refs):
    chunks, (images, keep, send, weights, text) = refs[:4], refs[4:]
    slab_weights(other, start, multiplier, offset, chunks, images, text, weights)
    slab_terms(other, images, weights, keep, send)


def own_kernel(*refs):
    terms_kernel(0, *refs)


def other_kernel(*refs):
    terms_kernel(1, *refs)


def pieces_kernel(*refs):
    chunks, square, pieces, (text, weights, grad) = refs[:8], refs[8:10], refs[10:14], refs[14:]
    for d, chunk in enumerate(chunks):
        text[CHUNK * d : CHUNK * d + CHUNK, :] = chunk[...]
    for slab in range(2):
        weights[ROWS * slab : ROWS * slab + ROWS, :] = square[slab][...]
    mine = lax.axis_index("t")
    grad[...] = turned_product(text, weights)
    for d, piece in enumerate(pieces):
        piece[...] = grad[window(ahead(mine, d), PART), :].astype(BF16)


def join_kernel(own, from_other, other, from_own, *outs):
    place = spot()[1]
    for d, out in enumerate(outs):
        rows = window(ahead(place, d), 4)
        out[:, :16, :] = (own[rows] + from_other[rows].astype(F32)).astype(out.dtype)
        out[:, 16:, :] = (other[rows] + from_own[rows].astype(F32)).astype(out.dtype)


def first_sum_kernel(own, one, two, three, *refs):
    outs, total = refs[:4], refs[4]
    place = spot()[2]
    total[...] = (own[...] + one[...].astype(F32)) + (two[...].astype(F32) + three[...].astype(F32))
    for d, out in enumerate(outs):
        out[...] = total[ahead(place, d)].astype(out.dtype)


def second_sum_kernel(start, own, one, two, three, keep, send, total):
    z_lo = lax.axis_index("zl")
    step = holder_of(start, 0)[0]
    total[...] = (own[...] + one[...].astype(F32)) + (two[...].astype(F32) + three[...].astype(F32))
    for slab, at in ((0, step), (1, 1 - step)):
        keep[at] = total[window(2 * slab + z_lo, 8), :]
        send[at] = total[window(2 * slab + 1 - z_lo, 8), :].astype(BF16)


def lay_copies(places, out, done):
    mine = lax.axis_index("t")
    run(
        [
            pltpu.make_async_copy(piece, out.at[:, window(back(mine, d), ROWS)], done.at[i])
            for i, (d, piece) in enumerate(places)
        ]
    )


def lay_near_kernel(own, one, three, out, done):
    lay_copies([(0, own), (1, one), (3, three)], out, done)


def lay_far_kernel(two, before, out, done):
    lay_copies([(2, two)], out, done)


def lay_near(own, one, three):
    return pl.pallas_call(
        lay_near_kernel,
        out_shape=like(PART, PEERS * ROWS),
        in_specs=[VMEM] * 3,
        out_specs=HBM,
        compiler_params=pltpu.CompilerParams(vmem_limit_bytes=4 << 20),
        scratch_shapes=[DMA((3,))],
    )(own, one, three)


def lay_far(two, before):
    return pl.pallas_call(
        lay_far_kernel,
        out_shape=like(PART, PEERS * ROWS),
        in_specs=[VMEM, HBM],
        out_specs=HBM,
        compiler_params=pltpu.CompilerParams(vmem_limit_bytes=4 << 20),
        scratch_shapes=[DMA((1,))],
        input_output_aliases={1: 0},
    )(two, before)


def per_device(pictures, captions, start, multiplier, offset):
    start, multiplier, offset = (value.reshape(1) for value in (start, multiplier, offset))
    scalars, scalar_specs = (start, multiplier, offset), [SMEM] * 3

    pictures = pictures.T
    near, one, three = call(cut_near_kernel, [like(PART, ROWS)] * 3, [HBM], [DMA((3,))], moved=2)(pictures)

    chunks = call(cut_text_kernel, [like(4, PIECE, D)] * 4, [HBM], [DMA((4,))], moved=2, vmem=60 << 20)(
        captions.reshape(4, 4, PIECE, D)
    )
    chunks = [chunks[0]] + [along(chunks[d], True, d) for d in (1, 2, 3)]
    one, three = shift(one, "t", 1, PEERS), shift(three, "t", 3, PEERS)
    pieces = call(first_pick_kernel, [like(PIECE, D)] * 4, [SMEM] + [VMEM] * 4)(start, *chunks)
    pieces = [pieces[0]] + [along(pieces[d], False, d) for d in (1, 2, 3)]
    piece = call(second_pick_kernel, like(PIECE, D), [SMEM] + [VMEM] * 4)(start, *pieces)
    there = shift(piece, "zl", 1, 2)
    there, one, three = lax.optimization_barrier((there, one, three))
    low, high = call(cut_far_kernel, [like(PART, HALF)] * 2, [HBM], [DMA((2,))])(pictures)
    low, high = shift(low, "t", 2, PEERS), shift(high, "t", 2, PEERS)
    piece = call(unit_rows_kernel, like(PIECE, D), [SMEM] + [VMEM] * 2)(start, piece, there)

    pieces = [piece] + [along(piece, False, d) for d in (1, 2, 3)]
    *pieces, low = lax.optimization_barrier((*pieces, low))
    chunk = call(gather_kernel, like(CHUNK, D), [VMEM] * 4)(*pieces)
    own = [chunk] + [along(chunk, True, d) for d in (1, 2, 3)]
    theirs = [shift(chunk, "c", 1, 2) for chunk in own]
    images = call(unit_columns_kernel, like(D, ROWS), [VMEM] * 5, moved=3)(near, one, three, low, high)

    text_scratch = pltpu.VMEM((ROWS, D), BF16)
    kept, sent, square = like(*OWNED, dtype=F32), like(*OWNED), like(ROWS, ROWS)
    keep_own, send_own, own_weights = call(
        own_kernel, [kept, sent, square], scalar_specs + [VMEM] * 5, [text_scratch], products=3, moved=8
    )(*scalars, *own, images)
    keep_other, send_other, weights = call(
        other_kernel, [kept, sent, square], scalar_specs + [VMEM] * 5, [text_scratch], products=2, moved=5
    )(*scalars, *theirs, images)
    pieces = call(
        pieces_kernel,
        [like(PART, ROWS)] * PEERS,
        [VMEM] * 10,
        [pltpu.VMEM((2 * ROWS, D), BF16), pltpu.VMEM((2 * ROWS, ROWS), BF16), pltpu.VMEM((D, ROWS), F32)],
        products=1,
        moved=5,
    )(*own, *theirs, own_weights, weights)
    *pieces, keep_own = lax.optimization_barrier((*pieces, keep_own))
    returned = [pieces[0]] + [shift(pieces[d], "t", d, PEERS) for d in (1, 2, 3)]

    parts = call(
        join_kernel, [like(4, PIECE, D, dtype=F32)] + [like(4, PIECE, D)] * 3, [VMEM] * 4, moved=4
    )(keep_own, shift(send_other, "c", 1, 2), keep_other, shift(send_own, "c", 1, 2))
    parts = [parts[0]] + [along(parts[d], True, d) for d in (1, 2, 3)]
    parts = call(
        first_sum_kernel,
        [like(PIECE, D, dtype=F32)] + [like(PIECE, D)] * 3,
        [VMEM] * 4,
        [pltpu.VMEM((4, PIECE, D), F32)],
    )(*parts)
    parts = [parts[0]] + [along(parts[d], False, d) for d in (1, 2, 3)]
    keep, send = call(
        second_sum_kernel, [like(2, 8, D, dtype=F32), like(2, 8, D)], [SMEM] + [VMEM] * 4, [pltpu.VMEM((PIECE, D), F32)]
    )(start, *parts)
    text_grad = keep + shift(send, "zl", 1, 2).astype(F32)
    image_grad = lay_far(returned[2], lay_near(returned[0], returned[1], returned[3]))
    return image_grad.T, text_grad[:, None]


def solution(mesh):
    names, sizes = zip(*SIZES)
    grid = Mesh(mesh.devices.reshape(sizes), names)
    return jax.shard_map(
        per_device,
        mesh=grid,
        in_specs=(P(DP, "t"), P(names, None), P(), P(), P()),
        out_specs=(P(DP, "t"), P(None, "t", DP, None)),
        check_vma=False,
    )
```
